256 devices in a mesh: pipe: 4 (over x), seq: 32 (over z, y), batch: 2 (over core).
Axes of the slice: x: 4, y: 4, z: 8, core: 2. Of those that a mesh axis runs over, the one named last changes fastest.
Arguments:
- latent_noise: float32 [4, 2, 512, 64], P('pipe', 'batch', 'seq'), may hold values from -6 to 6
- text_rows: bfloat16 [4, 2, 256, 4096], P(None, 'batch', None, 'seq'), may hold values from -6 to 6
- text_lengths: int32 [4, 2], P(None, 'batch'), may hold values from 32 to 256, as said below
- plan: int32 [3], replicated, may hold values from 1 to 1000, as said below
- context_weight: bfloat16 [4096, 1536], P('seq'), may hold values from -0.09375 to 0.09375
- w_embed: bfloat16 [64, 1536], replicated, may hold values from -0.75 to 0.75
- w_attention: bfloat16 [4, 1536, 4608], P('pipe', 'batch'), may hold values from -1 to 1
- w_project: bfloat16 [4, 1536, 1536], P('pipe', 'batch'), may hold values from -0.15625 to 0.15625
- w_modulate: bfloat16 [4, 256, 4608], P('pipe', 'batch'), may hold values from -0.375 to 0.375
- w_final: bfloat16 [1536, 64], replicated, may hold values from -0.15625 to 0.15625
Outputs:
- final_latent: float32 [4, 2, 512, 64], P('pipe', 'batch', 'seq')
The draws below stay inside these ranges and needn't reach their ends.
Inputs may be any that keep to these rules, and one draw needn't show every extreme that they name: `text_lengths`: at least one prompt has 256 live rows and one has 32. `plan`: strictly falling; the first entry is 1000 and the last is 1.
All inputs are finite; a program needn't handle non-finite values.
Results may differ from the reference program's by a relative error of at most 0.02.
Values may be sent and summed in bfloat16 or wider, within the bound.
No kernel may reach another device: no remote copies, remote signals or barrier semaphores. Data moves between devices by JAX's collectives and lax.ppermute only.
A program may use at most 128 MiB of HBM per device.

```python
import math
import jax
import jax.numpy as jnp
from jax import lax

D = 1536
HEADS = 16
HEAD_DIM = 96
T5W = 4096
LAT = 64
FREQ = 256
STEPS = 2
BLOCK_SECTIONS = 4
MB = 4
GROUPS = 2
IMG = 512
TXT = 256


def draw_text_lengths(key, part):
    prompt_count = MB * GROUPS
    first_key, second_key = jax.random.split(key)
    drawn = jax.random.randint(first_key, (prompt_count,), TXT // 8, TXT + 1)
    order = jax.random.permutation(second_key, prompt_count)
    drawn = drawn.at[order[0]].set(TXT).at[order[1]].set(TXT // 8)
    return drawn.reshape(MB, GROUPS).astype(jnp.int32)


def draw_plan(key, part):
    picked = jax.random.permutation(key, 998)[:STEPS - 1] + 2
    ordered = -jnp.sort(-picked)
    return jnp.concatenate([jnp.array([1000], dtype=jnp.int32), ordered.astype(jnp.int32), jnp.array([1], dtype=jnp.int32)])


def draw_w_attention(key, part):
    inner_width = HEADS * HEAD_DIM
    first_key = jax.random.fold_in(key, 0)
    drawn = jax.random.truncated_normal(first_key, -3.0, 3.0, (BLOCK_SECTIONS, D, 3 * inner_width), jnp.float32) / math.sqrt(D)
    return jnp.clip(drawn, -1.0, 1.0).astype(jnp.bfloat16)


def block_levels(key, shape, cuts, least, top_value):
    def one(dim, parts):
        draws = jax.random.uniform(jax.random.fold_in(jax.random.fold_in(key, 6), dim), (parts,), jnp.float32, least / len(cuts), top_value / len(cuts))
        return jnp.repeat(jnp.exp(draws), shape[dim] // parts).reshape((-1,) + (1,) * (len(shape) - dim - 1))

    level = one(*cuts[0])
    for cut in cuts[1:]:
        level = level * one(*cut)
    return level


def noise(own_key, dims, width, reach, cuts=(), held_as=jnp.bfloat16):
    values = width * jax.random.normal(own_key, dims, jnp.float32)
    if cuts:
        values = values * block_levels(own_key, dims, cuts, -0.22, 0.18)
    return jnp.clip(values, -reach, reach).astype(held_as)


def setup_inputs(seed: int = 0) -> dict:
    splits = jax.random.split(jax.random.key(seed), 11)
    return {
        "latent_noise": noise(splits[0], (MB, GROUPS, IMG, LAT), 1.0, 6.0, ((0, 4), (1, 2), (2, 32)), jnp.float32),
        "text_rows": noise(splits[1], (MB, GROUPS, TXT, T5W), 1.0, 6.0, ((1, 2), (3, 32))),
        "text_lengths": draw_text_lengths(jax.random.fold_in(splits[10], 71), 0),
        "plan": draw_plan(jax.random.fold_in(splits[10], 71), 0),
        "context_weight": noise(splits[4], (T5W, D), T5W ** -0.5, 0.09375, ((0, 32),)),
        "w_embed": noise(splits[5], (LAT, D), LAT ** -0.5, 0.75),
        "w_attention": draw_w_attention(jax.random.fold_in(splits[10], 71), 0),
        "w_project": noise(splits[7], (BLOCK_SECTIONS, HEADS * HEAD_DIM, D), (HEADS * HEAD_DIM) ** -0.5, 0.15625, ((0, 4), (1, 2))),
        "w_modulate": noise(splits[8], (BLOCK_SECTIONS, FREQ, 3 * D), FREQ ** -0.5, 0.375, ((0, 4), (1, 2))),
        "w_final": noise(splits[9], (D, LAT), D ** -0.5, 0.15625),
    }


epsilon = 1e-06

def layer_norm(hidden):
    values = hidden.astype(jnp.float32)
    center = values - lax.optimization_barrier(jnp.mean(values, axis=-1, keepdims=True))
    spread = lax.optimization_barrier(jnp.mean(center * center, axis=-1, keepdims=True))
    return center * lax.rsqrt(spread + epsilon)

def time_features(noise_level, feature_count):
    half_count = feature_count // 2
    wave_frequency = jnp.exp(-math.log(10000.0) * jnp.arange(half_count, dtype=jnp.float32) / half_count)
    angles = noise_level * wave_frequency
    return jnp.concatenate([jnp.cos(angles), jnp.sin(angles)]).astype(jnp.bfloat16)

def one_image(hidden, context, live_keys, modulation, attn_weight, proj_weight):
    model_width = hidden.shape[1]
    inner_width = proj_weight.shape[0]
    head_size = inner_width // HEADS
    image_patch_count = hidden.shape[0]
    mod_shift = modulation[:model_width]
    mod_scale = modulation[model_width:2 * model_width]
    mod_gate = modulation[2 * model_width:]
    normed = (layer_norm(hidden) * (1.0 + mod_scale) + mod_shift).astype(jnp.bfloat16)
    projected = jnp.dot(normed, attn_weight, preferred_element_type=jnp.float32).astype(jnp.bfloat16)
    text_pairs = jnp.dot(context, attn_weight[:, inner_width:], preferred_element_type=jnp.float32).astype(jnp.bfloat16)
    all_keys = jnp.concatenate([projected[:, inner_width:2 * inner_width], text_pairs[:, :inner_width]], 0)
    all_values = jnp.concatenate([projected[:, 2 * inner_width:], text_pairs[:, inner_width:]], 0)

    def heads_first(key_rows):
        return key_rows.reshape(key_rows.shape[0], HEADS, head_size).transpose(1, 0, 2).astype(jnp.float32)
    scores = jnp.einsum('hqc,hkc->hqk', heads_first(projected[:, :inner_width]), heads_first(all_keys)) * (1.0 / math.sqrt(head_size))
    key_mask = jnp.concatenate([jnp.ones((image_patch_count,), dtype=bool), live_keys])
    scores = jnp.where(key_mask[None, None, :], scores, -1e+30)
    highest = lax.optimization_barrier(jnp.max(scores, axis=-1, keepdims=True))
    exponents = jnp.exp(scores - highest)
    totals = lax.optimization_barrier(jnp.sum(exponents, axis=-1, keepdims=True))
    weights = (exponents / totals).astype(jnp.bfloat16)
    attended = jnp.einsum('hqk,hkc->hqc', weights.astype(jnp.float32), heads_first(all_values)).astype(jnp.bfloat16)
    merged_heads = attended.transpose(1, 0, 2).reshape(image_patch_count, inner_width)
    update = jnp.dot(merged_heads, proj_weight, preferred_element_type=jnp.float32)
    return (hidden.astype(jnp.float32) + mod_gate * update).astype(jnp.bfloat16)

def reference(latent_noise, text_rows, text_lengths, plan, context_weight, w_embed, w_attention, w_project, w_modulate, w_final):
    images = MB * GROUPS
    context = jnp.dot(text_rows.reshape(images * TXT, T5W), context_weight, preferred_element_type=jnp.float32).astype(jnp.bfloat16).reshape(images, TXT, D)
    live_text = jnp.arange(TXT)[None, :] < text_lengths.reshape(images, 1)
    latent = latent_noise.reshape(images, IMG, LAT)
    for step_index in range(STEPS):
        noise_level = plan[step_index].astype(jnp.float32)
        next_level = plan[step_index + 1].astype(jnp.float32)
        features = time_features(noise_level, FREQ)
        hidden = jnp.dot(latent.astype(jnp.bfloat16).reshape(images * IMG, LAT), w_embed, preferred_element_type=jnp.float32).astype(jnp.bfloat16).reshape(images, IMG, D)
        for section in range(BLOCK_SECTIONS):
            modulation = jnp.dot(features[None, :], w_modulate[section], preferred_element_type=jnp.float32)[0]
            attn_weight = w_attention[section]
            proj_weight = w_project[section]

            def apply_block(item, modulation=modulation, attn_weight=attn_weight, proj_weight=proj_weight):
                return one_image(item[0], item[1], item[2], modulation, attn_weight, proj_weight)
            hidden = lax.map(apply_block, (hidden, context, live_text))
        normed_out = layer_norm(hidden).astype(jnp.bfloat16)
        velocity = jnp.dot(normed_out.reshape(images * IMG, D), w_final, preferred_element_type=jnp.float32).reshape(images, IMG, LAT)
        latent = latent + (next_level - noise_level) / 1000.0 * velocity
    return latent.reshape(MB, GROUPS, IMG, LAT)
```

```python
import functools
import math

import jax
import jax.numpy as jnp
from jax import lax
from jax.experimental import pallas as pl
from jax.experimental.pallas import tpu as pltpu
from jax.sharding import Mesh, PartitionSpec as P

HEADS = 16
HEAD = 96
STEPS = 2
BLOCKS = 4
X, Z, Y, C = 4, 8, 4, 2
AXES = ("x", "z", "y", "c")
BF = jnp.bfloat16
F32 = jnp.float32
VMEM = 56 * 1024 * 1024

epsilon = 1e-06


def layer_norm(hidden):
    values = hidden.astype(F32)
    center = values - jnp.mean(values, axis=-1, keepdims=True)
    spread = jnp.mean(center * center, axis=-1, keepdims=True)
    return center * lax.rsqrt(spread + epsilon)


def time_features(noise_level, feature_count):
    half_count = feature_count // 2
    wave_frequency = jnp.exp(
        -math.log(10000.0) * jnp.arange(half_count, dtype=F32) / half_count
    )
    angles = noise_level * wave_frequency
    return jnp.concatenate([jnp.cos(angles), jnp.sin(angles)]).astype(BF)


def flat(x, z, y, c):
    return ((x * Z + z) * Y + y) * C + c


def move(value, pairs):
    return lax.ppermute(value, AXES, [(flat(*a), flat(*b)) for a, b in pairs])


def homes():
    return [(z // 2, z, z % 2) for z in range(Z)]


def product_kernel(core_ref, rows_ref, shift_ref, scale_ref, own_ref, other_ref, out_ref, normed, *, norm):
    half = own_ref.shape[0]
    total = rows_ref.shape[0]
    step = min(total, 128)

    @pl.when(pl.program_id(0) == 0)
    def _():
        def body(i, carry):
            rows = pl.ds(pl.multiple_of(i * step, step), step)
            values = rows_ref[rows, :].astype(F32)
            if norm:
                center = values - jnp.mean(values, axis=-1, keepdims=True)
                spread = jnp.mean(center * center, axis=-1, keepdims=True)
                values = center * lax.rsqrt(spread + epsilon)
                values = values * (1.0 + scale_ref[...]) + shift_ref[...]
            normed[rows, :] = values.astype(BF)
            return carry

        lax.fori_loop(0, total // step, body, 0)

    core = core_ref[0]
    mine = pl.ds(pl.multiple_of(core * half, 128), half)
    theirs = pl.ds(pl.multiple_of((1 - core) * half, 128), half)
    out_ref[...] = (
        jnp.dot(normed[:, mine], own_ref[...], preferred_element_type=F32)
        + jnp.dot(normed[:, theirs], other_ref[...], preferred_element_type=F32)
    ).astype(BF)


def product(core, rows, shift, scale, own, other, first, columns, norm, block=512):
    count, width = rows.shape
    half = own.shape[0]
    start = first // block
    return pl.pallas_call(
        functools.partial(product_kernel, norm=norm),
        grid=(columns // block,),
        in_specs=[
            pl.BlockSpec(memory_space=pltpu.SMEM),
            pl.BlockSpec((count, width), lambda i: (0, 0)),
            pl.BlockSpec((1, width), lambda i: (0, 0)),
            pl.BlockSpec((1, width), lambda i: (0, 0)),
            pl.BlockSpec((half, block), lambda i: (0, i + start)),
            pl.BlockSpec((half, block), lambda i: (0, i + start)),
        ],
        out_specs=pl.BlockSpec((count, block), lambda i: (0, i)),
        out_shape=jax.ShapeDtypeStruct((count, columns), BF),
        scratch_shapes=[pltpu.VMEM((count, width), BF)],
        compiler_params=pltpu.CompilerParams(vmem_limit_bytes=VMEM),
        name="product",
    )(core, rows, shift, scale, own, other)


def attention_kernel(
    core_ref, q_ref, k_ref, v_ref, kt_ref, vt_ref, bias_ref, hidden_ref, gate_ref, own_ref, other_ref, out_ref, attended
):
    rows = q_ref.shape[0]
    half = own_ref.shape[0]
    factor = math.log2(math.e) / math.sqrt(HEAD)
    lanes = lax.broadcasted_iota(jnp.int32, (1, 128), 1)
    wide = lax.broadcasted_iota(jnp.int32, (1, 256), 1)
    bias = bias_ref[...]
    contract = (((1,), (1,)), ((), ()))

    def group(g, carry):
        base = pl.multiple_of(g * 4 * HEAD, 128)
        outs = []
        for h in range(4):
            low, high = h * HEAD, (h + 1) * HEAD
            start, stop = low // 128 * 128, -(-high // 128) * 128
            width = stop - start
            window = pl.ds(pl.multiple_of(base + start, 128), width)
            index = lanes if width == 128 else wide
            mask = ((index >= low - start) & (index < high - start)).astype(F32).astype(BF)
            q = q_ref[:, window] * mask
            image = lax.dot_general(q, k_ref[:, window], contract, preferred_element_type=F32)
            text = lax.dot_general(q, kt_ref[:, window], contract, preferred_element_type=F32) + bias
            top = jnp.maximum(
                jnp.max(image, axis=-1, keepdims=True), jnp.max(text, axis=-1, keepdims=True)
            )
            image = jnp.exp2((image - top) * factor)
            text = jnp.exp2((text - top) * factor)
            total = jnp.sum(image, axis=-1, keepdims=True) + jnp.sum(text, axis=-1, keepdims=True)
            value = jnp.dot(image.astype(BF), v_ref[:, window], preferred_element_type=F32) + jnp.dot(
                text.astype(BF), vt_ref[:, window], preferred_element_type=F32
            )
            outs.append(value * (1.0 / total))
        tiles = (
            jnp.where(lanes < 96, outs[0], outs[1][:, :128]),
            jnp.where(lanes < 64, outs[1][:, 128:], outs[2][:, :128]),
            jnp.where(lanes < 32, outs[2][:, 128:], outs[3]),
        )
        for j, tile in enumerate(tiles):
            attended[:, pl.ds(pl.multiple_of(base + j * 128, 128), 128)] = tile.astype(BF)
        return carry

    lax.fori_loop(0, HEADS // 4, group, 0)
    core = core_ref[0]
    mine = pl.ds(pl.multiple_of(core * half, 128), half)
    theirs = pl.ds(pl.multiple_of((1 - core) * half, 128), half)
    update = jnp.dot(attended[:, mine], own_ref[...], preferred_element_type=F32) + jnp.dot(
        attended[:, theirs], other_ref[...], preferred_element_type=F32
    )
    out_ref[...] = (hidden_ref[...].astype(F32) + gate_ref[...] * update).astype(BF)


def attention(core, qkv, text, bias, hidden, gate, own, other, block=256):
    count, width = hidden.shape
    text_count = text.shape[0]
    half = own.shape[0]
    return pl.pallas_call(
        attention_kernel,
        grid=(count // block,),
        in_specs=[
            pl.BlockSpec(memory_space=pltpu.SMEM),
            pl.BlockSpec((block, width), lambda i: (i, 0)),
            pl.BlockSpec((count, width), lambda i: (0, 1)),
            pl.BlockSpec((count, width), lambda i: (0, 2)),
            pl.BlockSpec((text_count, width), lambda i: (0, 0)),
            pl.BlockSpec((text_count, width), lambda i: (0, 1)),
            pl.BlockSpec((1, text_count), lambda i: (0, 0)),
            pl.BlockSpec((block, width), lambda i: (i, 0)),
            pl.BlockSpec((1, width), lambda i: (0, 0)),
            pl.BlockSpec((half, width), lambda i: (0, 0)),
            pl.BlockSpec((half, width), lambda i: (0, 0)),
        ],
        out_specs=pl.BlockSpec((block, width), lambda i: (i, 0)),
        out_shape=jax.ShapeDtypeStruct((count, width), BF),
        scratch_shapes=[pltpu.VMEM((block, width), BF)],
        compiler_params=pltpu.CompilerParams(vmem_limit_bytes=VMEM),
        name="attention",
    )(core, qkv, qkv, qkv, text, text, bias, hidden, gate, own, other)


def on_device(
    latent_noise,
    text_rows,
    text_lengths,
    plan,
    context_weight,
    w_embed,
    w_attention,
    w_project,
    w_modulate,
    w_final,
):
    x, z, y, c = (lax.axis_index(name) for name in AXES)
    width = w_embed.shape[1]
    latent_width = latent_noise.shape[3]
    patches = latent_noise.shape[2] * Z * Y
    text_total = text_rows.shape[2]
    core = jnp.reshape(c, (1,)).astype(jnp.int32)
    image = z // 2

    across = [((a, b, 0, 1 - b % 2), (a, b, 0, b % 2)) for a in range(X) for b in range(Z)]
    attn_own, proj_own, mod_own = w_attention[0], w_project[0], w_modulate[0]
    levels = plan.astype(F32)
    features = jnp.stack([time_features(levels[k], 2 * mod_own.shape[0]) for k in range(STEPS)])
    features = lax.dynamic_slice_in_dim(features, c * mod_own.shape[0], mod_own.shape[0], 1)
    modulation = jnp.dot(features, mod_own, preferred_element_type=F32)

    text = lax.dynamic_index_in_dim(text_rows[:, 0], x, 0, keepdims=False)
    partial = jnp.dot(text, context_weight, preferred_element_type=F32).astype(BF)
    quarter = text_total // Y
    parts = lax.all_to_all(
        partial.reshape(Y, quarter, width), "y", split_axis=0, concat_axis=0, tiled=True
    )
    summed = jnp.sum(parts.astype(F32), axis=0)
    rows_here = latent_noise.shape[2]
    latent = latent_noise[0, 0].reshape(-1)
    high = latent.astype(BF)
    low = (latent - high.astype(F32)).astype(BF)
    carried = -(-latent.size // width) * width
    pad = lambda value: jnp.pad(value, (0, carried - value.size)).reshape(-1, width)
    extra = jnp.concatenate([pad(high), pad(low)], 0)
    extra_rows = extra.shape[0]
    message = jnp.concatenate([summed.astype(BF), extra], 0)
    total = summed
    here = 2 * x + c
    pieces = jnp.zeros((Z, extra_rows, width), BF)
    pieces = lax.dynamic_update_index_in_dim(pieces, extra, here % Z, 0)
    for k in range(1, Z):
        got = move(
            message,
            [
                ((a, (2 * a + d + k) % Z, b, d), (a, 2 * a + d, b, d))
                for a in range(X)
                for b in range(Y)
                for d in range(C)
            ],
        )
        total = total + got[:quarter].astype(F32)
        pieces = lax.dynamic_update_index_in_dim(pieces, got[quarter:], (here + k) % Z, 0)
    message = jnp.concatenate([total.astype(BF), pieces.reshape(Z * extra_rows, width)], 0)
    shared = jnp.where(x == image, message, jnp.zeros_like(message))
    for k in range(1, X):
        shared = shared + move(
            message,
            [((m, b, a, d), ((m + k) % X, b, a, d)) for m, b, d in homes() for a in range(Y)],
        )
    gathered = [shared]
    for k in range(1, Y):
        gathered.append(move(shared, [((a, b, k, d), (a, b, 0, d)) for a in range(X) for _, b, d in homes()]))
    context = jnp.concatenate([part[:quarter] for part in gathered], 0)

    def latent_of(part):
        flat_rows = part[quarter:].reshape(Z, 2, carried)[:, :, : rows_here * latent_width]
        return flat_rows.reshape(Z, 2, rows_here, latent_width)

    latents = jnp.stack([latent_of(part) for part in gathered], 1)
    latent_high = latents[:, :, 0].reshape(patches, latent_width)
    latent_low = latents[:, :, 1].reshape(patches, latent_width)
    latent = latent_high.astype(F32) + latent_low.astype(F32)

    attn_other = move(attn_own, across)
    proj_other = move(proj_own, across)
    modulation = modulation + move(modulation, across)

    length = jnp.sum(jnp.where(jnp.arange(X) == image, text_lengths[:, 0], 0))
    bias = jnp.where(jnp.arange(text_total) < length, 0.0, -1e30).astype(F32)[None, :]
    nothing = jnp.zeros((1, width), F32)
    pairs_text = product(
        core, context, nothing, nothing, attn_own, attn_other, width, 2 * width, False
    )

    hidden = jnp.dot(latent_high, w_embed, preferred_element_type=F32).astype(BF)
    for turn in range(STEPS * BLOCKS):
        step, block = divmod(turn, BLOCKS)
        shift = modulation[step : step + 1, :width]
        scale = modulation[step : step + 1, width : 2 * width]
        gate = modulation[step : step + 1, 2 * width :]
        qkv = product(core, hidden, shift, scale, attn_own, attn_other, 0, 3 * width, True)
        hidden = attention(core, qkv, pairs_text, bias, hidden, gate, proj_own, proj_other)
        if block < BLOCKS - 1:
            hidden = move(
                hidden, [((block, b, 0, d), (block + 1, b, 0, d)) for _, b, d in homes()]
            )
        else:
            velocity = jnp.dot(
                layer_norm(hidden).astype(BF), w_final, preferred_element_type=F32
            )
            latent = latent + (levels[step + 1] - levels[step]) / 1000.0 * velocity
            if step < STEPS - 1:
                first = move(
                    latent.astype(BF), [((block, b, 0, d), (0, b, 0, d)) for _, b, d in homes()]
                )
                hidden = jnp.dot(first, w_embed, preferred_element_type=F32).astype(BF)

    last = BLOCKS - 1
    moved = move(latent, [((last, b, 0, d), (m, b, 0, d)) for m, b, d in homes() if m != last])
    latent = jnp.where(x == last, latent, moved)
    spread = lax.all_to_all(
        latent.reshape(Z * Y, rows_here, latent_width),
        ("z", "y"),
        split_axis=0,
        concat_axis=0,
        tiled=True,
    )
    mine = lax.dynamic_index_in_dim(spread, here * Y, 0, keepdims=False)
    return mine.reshape(latent_noise.shape)


def solution(mesh):
    inner = Mesh(mesh.devices.reshape(X, Z, Y, C), AXES)
    seq = ("z", "y")
    placed = (
        P("x", "c", seq, None),
        P(None, "c", None, seq),
        P(None, "c"),
        P(),
        P(seq, None),
        P(),
        P("x", "c", None),
        P("x", "c", None),
        P("x", "c", None),
        P(),
    )
    return jax.shard_map(
        on_device,
        mesh=inner,
        in_specs=placed,
        out_specs=P("x", "c", seq, None),
        check_vma=False,
    )
```

```python
import functools
import math

import jax
import jax.numpy as jnp
from jax import lax
from jax.experimental import pallas as pl
from jax.experimental.pallas import tpu as pltpu
from jax.sharding import Mesh, PartitionSpec as P

HEADS = 16
HEAD = 96
STEPS = 2
BLOCKS = 4
X, Z, Y, C = 4, 8, 4, 2
AXES = ("x", "z", "y", "c")
BF = jnp.bfloat16
F32 = jnp.float32
VMEM = 24 * 1024 * 1024
SPAN = 768
CHUNKS = 2

epsilon = 1e-06


def layer_norm(hidden):
    values = hidden.astype(F32)
    center = values - jnp.mean(values, axis=-1, keepdims=True)
    spread = jnp.mean(center * center, axis=-1, keepdims=True)
    return center * lax.rsqrt(spread + epsilon)


def time_features(noise_level, feature_count):
    half_count = feature_count // 2
    wave_frequency = jnp.exp(
        -math.log(10000.0) * jnp.arange(half_count, dtype=F32) / half_count
    )
    angles = noise_level * wave_frequency
    return jnp.concatenate([jnp.cos(angles), jnp.sin(angles)]).astype(BF)


def flat(x, z, y, c):
    return ((x * Z + z) * Y + y) * C + c


def move(value, pairs):
    return lax.ppermute(value, AXES, [(flat(*a), flat(*b)) for a, b in pairs])


def homes():
    return [(z // 2, z, z % 2) for z in range(Z)]


def whole():
    return pl.BlockSpec(memory_space=pltpu.VMEM)


def params():
    return pltpu.CompilerParams(vmem_limit_bytes=VMEM)


def product_kernel(core_ref, first_ref, second_ref, shift_ref, scale_ref, own_ref, other_ref, out_ref, normed, *, norm, column):
    half = own_ref.shape[0]
    count = first_ref.shape[0]
    step = min(count, 64)

    for place, ref in enumerate((first_ref, second_ref)):

        def body(i, carry, ref=ref, place=place):
            values = ref[pl.ds(pl.multiple_of(i * step, step), step), :]
            if norm:
                values = values.astype(F32)
                center = values - jnp.mean(values, axis=-1, keepdims=True)
                spread = jnp.mean(center * center, axis=-1, keepdims=True)
                values = center * lax.rsqrt(spread + epsilon)
                values = (values * (1.0 + scale_ref[...]) + shift_ref[...]).astype(BF)
            normed[pl.ds(pl.multiple_of(place * count + i * step, step), step), :] = values
            return carry

        lax.fori_loop(0, count // step, body, 0, unroll=True)

    core = core_ref[0]
    mine = normed[:, pl.ds(pl.multiple_of(core * half, 128), half)]
    theirs = normed[:, pl.ds(pl.multiple_of((1 - core) * half, 128), half)]
    for i in range(out_ref.shape[1] // SPAN):
        there = slice(i * SPAN, (i + 1) * SPAN)
        here = slice(column + i * SPAN, column + (i + 1) * SPAN)
        out_ref[:, there] = (
            jnp.dot(mine, own_ref[:, here], preferred_element_type=F32)
            + jnp.dot(theirs, other_ref[:, here], preferred_element_type=F32)
        ).astype(BF)


def product(core, first, second, shift, scale, own, other, column, norm):
    count, width = first.shape
    columns = own.shape[1] - column
    return pl.pallas_call(
        functools.partial(product_kernel, norm=norm, column=column),
        in_specs=[pl.BlockSpec(memory_space=pltpu.SMEM)] + [whole()] * 6,
        out_specs=whole(),
        out_shape=jax.ShapeDtypeStruct((2 * count, columns), BF),
        scratch_shapes=[pltpu.VMEM((2 * count, width), BF)],
        compiler_params=params(),
        name="product",
    )(core, first, second, shift, scale, own, other)


def attention_kernel(*refs, query):
    *blocks, text_ref, bias_ref, own_ref, other_ref = refs
    rows = own_ref.shape[0]
    inner = own_ref.shape[1]
    factor = math.log2(math.e) / math.sqrt(HEAD)
    lanes = lax.broadcasted_iota(jnp.int32, (1, 128), 1)
    wide = lax.broadcasted_iota(jnp.int32, (1, 256), 1)
    bias = bias_ref[...]
    contract = (((1,), (1,)), ((), ()))

    def group(g, carry):
        base = pl.multiple_of(g * 4 * HEAD, 128)
        outs = []
        for h in range(4):
            low, high = h * HEAD, (h + 1) * HEAD
            start, stop = low // 128 * 128, -(-high // 128) * 128
            width = stop - start

            def window(offset):
                return pl.ds(pl.multiple_of(base + start + offset, 128), width)

            index = lanes if width == 128 else wide
            mask = ((index >= low - start) & (index < high - start)).astype(F32).astype(BF)
            q = blocks[query][:, window(0)] * mask
            scores = [
                lax.dot_general(q, ref[:, window(inner)], contract, preferred_element_type=F32)
                for ref in blocks
            ]
            scores.append(
                lax.dot_general(q, text_ref[:, window(0)], contract, preferred_element_type=F32)
                + bias
            )
            top = functools.reduce(
                jnp.maximum, [jnp.max(part, axis=-1, keepdims=True) for part in scores]
            )
            scores = [jnp.exp2((part - top) * factor) for part in scores]
            total = sum(jnp.sum(part, axis=-1, keepdims=True) for part in scores)
            value = jnp.dot(
                scores[-1].astype(BF), text_ref[:, window(inner)], preferred_element_type=F32
            )
            for part, ref in zip(scores[:-1], blocks):
                value = value + jnp.dot(
                    part.astype(BF), ref[:, window(2 * inner)], preferred_element_type=F32
                )
            outs.append(value * (1.0 / total))
        tiles = (
            jnp.where(lanes < 96, outs[0], outs[1][:, :128]),
            jnp.where(lanes < 64, outs[1][:, 128:], outs[2][:, :128]),
            jnp.where(lanes < 32, outs[2][:, 128:], outs[3]),
        )
        for j, tile in enumerate(tiles):
            there = pl.ds(pl.multiple_of(base + j * 128, 128), 128)
            own_ref[:, there] = tile[:rows].astype(BF)
            other_ref[:, there] = tile[rows:].astype(BF)
        return carry

    lax.fori_loop(0, inner // (4 * HEAD), group, 0)


def attention(blocks, text, bias, query):
    count = blocks[query].shape[0] // 2
    inner = blocks[query].shape[1] // 3
    shape = jax.ShapeDtypeStruct((count, inner), BF)
    return pl.pallas_call(
        functools.partial(attention_kernel, query=query),
        in_specs=[whole()] * (len(blocks) + 2),
        out_specs=(whole(), whole()),
        out_shape=(shape, shape),
        compiler_params=params(),
        name="attention",
    )(*blocks, text, bias)


def update_kernel(first_ref, second_ref, hidden_ref, gate_ref, own_ref, other_ref, out_ref):
    update = jnp.dot(first_ref[...], own_ref[...], preferred_element_type=F32) + jnp.dot(
        second_ref[...], other_ref[...], preferred_element_type=F32
    )
    out_ref[...] = (hidden_ref[...].astype(F32) + gate_ref[...] * update).astype(BF)


def updated(first, second, hidden, gate, own, other):
    return pl.pallas_call(
        update_kernel,
        in_specs=[whole()] * 6,
        out_specs=whole(),
        out_shape=jax.ShapeDtypeStruct(hidden.shape, BF),
        compiler_params=params(),
        name="update",
    )(first, second, hidden, gate, own, other)


def on_device(
    latent_noise,
    text_rows,
    text_lengths,
    plan,
    context_weight,
    w_embed,
    w_attention,
    w_project,
    w_modulate,
    w_final,
):
    x, z, y, c = (lax.axis_index(name) for name in AXES)
    width = w_embed.shape[1]
    inner = w_project.shape[1]
    latent_width = latent_noise.shape[3]
    rows_here = latent_noise.shape[2]
    patches = rows_here * Z * Y
    text_total = text_rows.shape[2]
    core = jnp.reshape(c, (1,)).astype(jnp.int32)
    image = z // 2

    def swap(value):
        return move(
            value, [((a, b, 0, d), (a, b, 0, 1 - d)) for a in range(X) for b in range(Z) for d in range(C)]
        )

    def hop(value, source, target):
        return move(
            value, [((source, b, 0, d), (target, b, 0, d)) for b in range(Z) for d in range(C)]
        )

    def columns_of(who):
        return jnp.concatenate(
            [
                lax.dynamic_slice_in_dim(w_attention[0], part * width + who * inner, inner, 1)
                for part in range(3)
            ],
            1,
        )

    levels = plan.astype(F32)
    mod_rows = w_modulate.shape[1]
    features = jnp.stack([time_features(levels[k], C * mod_rows) for k in range(STEPS)])
    features = lax.dynamic_slice_in_dim(features, c * mod_rows, mod_rows, 1)

    text = lax.dynamic_index_in_dim(text_rows[:, 0], x, 0, keepdims=False)
    partial = jnp.dot(text, context_weight, preferred_element_type=F32).astype(BF)
    quarter = text_total // Y
    eighth = quarter // Z
    parts = lax.all_to_all(
        partial.reshape(Y, quarter, width), "y", split_axis=0, concat_axis=0, tiled=True
    )
    summed = jnp.sum(parts.astype(F32), axis=0).astype(BF)
    parts = lax.all_to_all(
        summed.reshape(Z, eighth, width), "z", split_axis=0, concat_axis=0, tiled=True
    )
    summed = jnp.sum(parts.astype(F32), axis=0).astype(BF)

    latent = latent_noise[0, 0].reshape(-1)
    high = latent.astype(BF)
    low = (latent - high.astype(F32)).astype(BF)
    both = jnp.concatenate([high, low])
    tail = -(-both.size // width)
    piece = jnp.concatenate(
        [summed, jnp.pad(both, (0, tail * width - both.size)).reshape(tail, width)], 0
    )
    held = eighth + tail
    shared = lax.all_to_all(
        jnp.broadcast_to(piece[None], (X, held, width)), "x", split_axis=0, concat_axis=0, tiled=True
    )
    shared = jnp.repeat(shared, Z // X, axis=0)
    shared = lax.all_to_all(shared, "z", split_axis=0, concat_axis=0, tiled=True)
    pieces = [shared.reshape(Z * held, width)]
    for k in range(1, Y):
        pieces.append(
            move(
                pieces[0],
                [((a, b, k, b % C), (a, b, 0, b % C)) for a in range(X) for b in range(Z)],
            )
        )
    pieces = jnp.stack(pieces).reshape(Y, Z, held, width)
    lead = z % C
    context = pieces[:, :, :eighth].reshape(text_total, width)
    latents = pieces[:, :, eighth:].reshape(Y, Z, tail * width)[:, :, : both.size]
    latents = latents.reshape(Y, Z, 2, rows_here, latent_width)
    latents = jnp.transpose(latents, (2, 1, 0, 3, 4)).reshape(2, patches, latent_width)
    part_rows = patches // C
    theirs = lax.dynamic_slice_in_dim(latents, (1 - c) * part_rows, part_rows, 1)
    latents = lax.dynamic_slice_in_dim(latents, c * part_rows, part_rows, 1)
    sent_context, sent_latents = swap(context), swap(theirs)
    context = jnp.where(c == lead, context, sent_context)
    latents = jnp.where(c == lead, latents, sent_latents)
    latent = latents[0].astype(F32) + latents[1].astype(F32)

    modulation = jnp.dot(features, w_modulate[0], preferred_element_type=F32)
    attn_own, proj_own = columns_of(c), w_project[0]
    attn_other = swap(columns_of(1 - c))
    proj_other = swap(proj_own)
    modulation = modulation + swap(modulation)

    length = jnp.sum(jnp.where(jnp.arange(X) == image, text_lengths[:, 0], 0))
    other_length = swap(length.astype(F32).reshape(1, 1) + jnp.zeros((8, 128), F32))[0, 0]
    length = jnp.where(c == lead, length.astype(F32), other_length)
    bias = jnp.where(jnp.arange(text_total) < length, 0.0, -1e30).astype(F32)[None, :]

    nothing = jnp.zeros((1, width), F32)
    keys = product(
        core,
        context[: text_total // 2],
        context[text_total // 2 :],
        nothing,
        nothing,
        attn_own,
        attn_other,
        inner,
        False,
    )

    rows = part_rows // CHUNKS

    def embedded(value):
        return jnp.dot(value, w_embed, preferred_element_type=F32).astype(BF)

    hidden = [embedded(latents[0, i * rows : (i + 1) * rows]) for i in range(CHUNKS)]
    for turn in range(STEPS * BLOCKS):
        step, block = divmod(turn, BLOCKS)
        shift = modulation[step : step + 1, :width]
        scale = modulation[step : step + 1, width : 2 * width]
        gate = modulation[step : step + 1, 2 * width :]
        projected = [
            product(core, part, swap(part), shift, scale, attn_own, attn_other, 0, True)
            for part in hidden
        ]
        following = []
        for i in range(CHUNKS):
            first, second = attention(projected, keys, bias, i)
            part = updated(first, swap(second), hidden[i], gate, proj_own, proj_other)
            if block < BLOCKS - 1:
                part = hop(part, block, block + 1)
            following.append(part)
        hidden = following
        if block == BLOCKS - 1:
            final = jnp.concatenate(hidden, 0)
            velocity = jnp.dot(
                layer_norm(final).astype(BF), w_final, preferred_element_type=F32
            )
            latent = latent + (levels[step + 1] - levels[step]) / 1000.0 * velocity
            if step < STEPS - 1:
                start = hop(latent.astype(BF), block, 0)
                hidden = [embedded(start[i * rows : (i + 1) * rows]) for i in range(CHUNKS)]

    last = BLOCKS - 1
    latent = latent.reshape(part_rows * latent_width // 128, 128)
    across = swap(latent)
    latent = jnp.where(
        c == 0, jnp.concatenate([latent, across], 0), jnp.concatenate([across, latent], 0)
    )
    moved = move(latent, [((last, b, 0, d), (m, b, 0, d)) for m, b, d in homes() if m != last])
    latent = jnp.where(x == last, latent, moved)
    spread = lax.all_to_all(
        latent.reshape(Z * Y, rows_here * latent_width // 128, 128),
        ("z", "y"),
        split_axis=0,
        concat_axis=0,
        tiled=True,
    )
    mine = lax.dynamic_index_in_dim(spread, (2 * x + c) * Y, 0, keepdims=False)
    return mine.reshape(latent_noise.shape)


def solution(mesh):
    inner = Mesh(mesh.devices.reshape(X, Z, Y, C), AXES)
    seq = ("z", "y")
    placed = (
        P("x", "c", seq, None),
        P(None, "c", None, seq),
        P(None, "c"),
        P(),
        P(seq, None),
        P(),
        P("x", "c", None),
        P("x", "c", None),
        P("x", "c", None),
        P(),
    )
    return jax.shard_map(
        on_device,
        mesh=inner,
        in_specs=placed,
        out_specs=P("x", "c", seq, None),
        check_vma=False,
    )
```

```python
import functools
import math

import jax
import jax.numpy as jnp
from jax import lax
from jax.experimental import pallas as pl
from jax.experimental.pallas import tpu as pltpu
from jax.sharding import Mesh, PartitionSpec as P

HEADS = 16
HEAD = 96
STEPS = 2
BLOCKS = 4
X, Z, Y, C = 4, 8, 4, 2
AXES = ("x", "z", "y", "c")
BF = jnp.bfloat16
F32 = jnp.float32
VMEM = 26 * 1024 * 1024
SPAN = 768
CHUNKS = 4
TOGETHER = 2

epsilon = 1e-06


def layer_norm(hidden):
    values = hidden.astype(F32)
    center = values - jnp.mean(values, axis=-1, keepdims=True)
    spread = jnp.mean(center * center, axis=-1, keepdims=True)
    return center * lax.rsqrt(spread + epsilon)


def time_features(noise_level, feature_count):
    half_count = feature_count // 2
    wave_frequency = jnp.exp(
        -math.log(10000.0) * jnp.arange(half_count, dtype=F32) / half_count
    )
    angles = noise_level * wave_frequency
    return jnp.concatenate([jnp.cos(angles), jnp.sin(angles)]).astype(BF)


def flat(x, z, y, c):
    return ((x * Z + z) * Y + y) * C + c


def move(value, pairs):
    return lax.ppermute(value, AXES, [(flat(*a), flat(*b)) for a, b in pairs])


def homes():
    return [(z // 2, z, z % 2) for z in range(Z)]


def whole():
    return pl.BlockSpec(memory_space=pltpu.VMEM)


def scalar():
    return pl.BlockSpec(memory_space=pltpu.SMEM)


def params():
    return pltpu.CompilerParams(vmem_limit_bytes=VMEM)


def joined_kernel(core_ref, own_ref, other_ref, out_ref, sems):
    half = own_ref.shape[0]
    core = core_ref[0]
    copies = (
        pltpu.make_async_copy(
            own_ref, out_ref.at[pl.ds(pl.multiple_of(core * half, 16), half), :], sems.at[0]
        ),
        pltpu.make_async_copy(
            other_ref, out_ref.at[pl.ds(pl.multiple_of((1 - core) * half, 16), half), :], sems.at[1]
        ),
    )
    for copy in copies:
        copy.start()
    for copy in copies:
        copy.wait()


def joined(core, own, other):
    half, columns = own.shape
    return pl.pallas_call(
        joined_kernel,
        in_specs=[scalar(), pl.BlockSpec(memory_space=pl.ANY), pl.BlockSpec(memory_space=pl.ANY)],
        out_specs=whole(),
        out_shape=jax.ShapeDtypeStruct((2 * half, columns), BF),
        scratch_shapes=[pltpu.SemaphoreType.DMA((2,))],
        compiler_params=params(),
        name="joined",
    )(core, own, other)


def product_kernel(rows_ref, shift_ref, scale_ref, weight_ref, out_ref, normed, *, norm, column):
    count = rows_ref.shape[0]
    step = min(count, 64)
    if norm:

        def body(i, carry):
            there = pl.ds(pl.multiple_of(i * step, step), step)
            values = rows_ref[there, :].astype(F32)
            center = values - jnp.mean(values, axis=-1, keepdims=True)
            spread = jnp.mean(center * center, axis=-1, keepdims=True)
            values = center * lax.rsqrt(spread + epsilon)
            normed[there, :] = (values * (1.0 + scale_ref[...]) + shift_ref[...]).astype(BF)
            return carry

        lax.fori_loop(0, count // step, body, 0, unroll=True)
        source = normed
    else:
        source = rows_ref
    for i in range(out_ref.shape[1] // SPAN):
        there = slice(i * SPAN, (i + 1) * SPAN)
        here = slice(column + i * SPAN, column + (i + 1) * SPAN)
        out_ref[:, there] = jnp.dot(
            source[...], weight_ref[:, here], preferred_element_type=F32
        ).astype(BF)


def product(rows, shift, scale, weight, column, norm):
    count, width = rows.shape
    columns = weight.shape[1] - column
    return pl.pallas_call(
        functools.partial(product_kernel, norm=norm, column=column),
        in_specs=[whole()] * 4,
        out_specs=whole(),
        out_shape=jax.ShapeDtypeStruct((count, columns), BF),
        scratch_shapes=[pltpu.VMEM((count, width), BF)],
        compiler_params=params(),
        name="product",
    )(rows, shift, scale, weight)


def attention_kernel(*refs, queries, blocks):
    projected, refs = refs[:blocks], refs[blocks:]
    text_ref, bias_ref, gate_ref, weight_ref, *refs = refs
    hidden_refs, out_refs, attended = refs[: len(queries)], refs[len(queries) : -1], refs[-1]
    inner = weight_ref.shape[0]
    factor = math.log2(math.e) / math.sqrt(HEAD)
    lanes = lax.broadcasted_iota(jnp.int32, (1, 128), 1)
    wide = lax.broadcasted_iota(jnp.int32, (1, 256), 1)
    bias = bias_ref[...]
    contract = (((1,), (1,)), ((), ()))

    def group(g, carry):
        base = pl.multiple_of(g * 4 * HEAD, 128)
        outs = []
        for h in range(4):
            low, high = h * HEAD, (h + 1) * HEAD
            start, stop = low // 128 * 128, -(-high // 128) * 128
            width = stop - start

            def window(refs, offset):
                there = pl.ds(pl.multiple_of(base + start + offset, 128), width)
                return jnp.concatenate([ref[:, there] for ref in refs], 0)

            index = lanes if width == 128 else wide
            mask = ((index >= low - start) & (index < high - start)).astype(F32).astype(BF)
            q = window([projected[i] for i in queries], 0) * mask
            image = lax.dot_general(
                q, window(projected, inner), contract, preferred_element_type=F32
            )
            text = lax.dot_general(
                q, window([text_ref], 0), contract, preferred_element_type=F32
            )
            text = text + bias
            top = jnp.maximum(
                jnp.max(image, axis=-1, keepdims=True), jnp.max(text, axis=-1, keepdims=True)
            )
            image = jnp.exp2((image - top) * factor)
            text = jnp.exp2((text - top) * factor)
            total = jnp.sum(image, axis=-1, keepdims=True) + jnp.sum(text, axis=-1, keepdims=True)
            value = jnp.dot(
                image.astype(BF), window(projected, 2 * inner), preferred_element_type=F32
            ) + jnp.dot(
                text.astype(BF), window([text_ref], inner), preferred_element_type=F32
            )
            outs.append(value * (1.0 / total))
        tiles = (
            jnp.where(lanes < 96, outs[0], outs[1][:, :128]),
            jnp.where(lanes < 64, outs[1][:, 128:], outs[2][:, :128]),
            jnp.where(lanes < 32, outs[2][:, 128:], outs[3]),
        )
        for j, tile in enumerate(tiles):
            attended[:, pl.ds(pl.multiple_of(base + j * 128, 128), 128)] = tile.astype(BF)
        return carry

    lax.fori_loop(0, inner // (4 * HEAD), group, 0)
    for i in range(weight_ref.shape[1] // SPAN):
        there = slice(i * SPAN, (i + 1) * SPAN)
        update = gate_ref[:, there] * jnp.dot(
            attended[...], weight_ref[:, there], preferred_element_type=F32
        )
        done = 0
        for hidden_ref, out_ref in zip(hidden_refs, out_refs):
            count = hidden_ref.shape[0]
            part = update[done : done + count]
            out_ref[:, there] = (hidden_ref[:, there].astype(F32) + part).astype(BF)
            done += count


def attention(projected, text, bias, gate, weight, hidden, queries):
    hidden = [hidden[i] for i in queries]
    rows = sum(part.shape[0] for part in hidden)
    return pl.pallas_call(
        functools.partial(attention_kernel, queries=queries, blocks=len(projected)),
        in_specs=[whole()] * (len(projected) + 4 + len(hidden)),
        out_specs=[whole()] * len(hidden),
        out_shape=[jax.ShapeDtypeStruct(part.shape, BF) for part in hidden],
        scratch_shapes=[pltpu.VMEM((rows, weight.shape[0]), BF)],
        compiler_params=params(),
        name="attention",
    )(*projected, text, bias, gate, weight, *hidden)


def on_device(
    latent_noise,
    text_rows,
    text_lengths,
    plan,
    context_weight,
    w_embed,
    w_attention,
    w_project,
    w_modulate,
    w_final,
):
    x, z, y, c = (lax.axis_index(name) for name in AXES)
    width = w_embed.shape[1]
    latent_width = latent_noise.shape[3]
    rows_here = latent_noise.shape[2]
    patches = rows_here * Z * Y
    text_total = text_rows.shape[2]
    core = jnp.reshape(c, (1,)).astype(jnp.int32)
    image = z // 2

    def across(value):
        return move(
            value, [((a, b, 0, 1 - b % C), (a, b, 0, b % C)) for a in range(X) for b in range(Z)]
        )

    def hop(value, source, target):
        return move(value, [((source, b, 0, d), (target, b, 0, d)) for _, b, d in homes()])

    attn_weight = joined(core, w_attention[0], across(w_attention[0]))
    proj_weight = joined(core, w_project[0], across(w_project[0]))
    levels = plan.astype(F32)
    mod_rows = w_modulate.shape[1]
    features = jnp.stack([time_features(levels[k], C * mod_rows) for k in range(STEPS)])
    features = lax.dynamic_slice_in_dim(features, c * mod_rows, mod_rows, 1)
    modulation = jnp.dot(features, w_modulate[0], preferred_element_type=F32)
    modulation = modulation + across(modulation)

    text = lax.dynamic_index_in_dim(text_rows[:, 0], x, 0, keepdims=False)
    partial = jnp.dot(text, context_weight, preferred_element_type=F32).astype(BF)
    quarter = text_total // Y
    eighth = quarter // Z
    parts = lax.all_to_all(
        partial.reshape(Y, quarter, width), "y", split_axis=0, concat_axis=0, tiled=True
    )
    summed = jnp.sum(parts.astype(F32), axis=0).astype(BF)
    parts = lax.all_to_all(
        summed.reshape(Z, eighth, width), "z", split_axis=0, concat_axis=0, tiled=True
    )
    summed = jnp.sum(parts.astype(F32), axis=0).astype(BF)

    latent = latent_noise[0, 0].reshape(-1)
    high = latent.astype(BF)
    low = (latent - high.astype(F32)).astype(BF)
    both = jnp.concatenate([high, low])
    tail = -(-both.size // width)
    piece = jnp.concatenate(
        [summed, jnp.pad(both, (0, tail * width - both.size)).reshape(tail, width)], 0
    )
    held = eighth + tail
    shared = lax.all_to_all(
        jnp.broadcast_to(piece[None], (X, held, width)), "x", split_axis=0, concat_axis=0, tiled=True
    )
    shared = jnp.repeat(shared, Z // X, axis=0)
    shared = lax.all_to_all(shared, "z", split_axis=0, concat_axis=0, tiled=True)
    pieces = [shared.reshape(Z * held, width)]
    for k in range(1, Y):
        pieces.append(
            move(
                pieces[0],
                [((a, b, k, b % C), (a, b, 0, b % C)) for a in range(X) for b in range(Z)],
            )
        )
    pieces = jnp.stack(pieces).reshape(Y, Z, held, width)
    context = pieces[:, :, :eighth].reshape(text_total, width)
    latents = pieces[:, :, eighth:].reshape(Y, Z, tail * width)[:, :, : both.size]
    latents = latents.reshape(Y, Z, 2, rows_here, latent_width)
    latents = jnp.transpose(latents, (2, 1, 0, 3, 4)).reshape(2, patches, latent_width)
    latent = latents[0].astype(F32) + latents[1].astype(F32)

    length = jnp.sum(jnp.where(jnp.arange(X) == image, text_lengths[:, 0], 0))
    bias = jnp.where(jnp.arange(text_total) < length, 0.0, -1e30).astype(F32)[None, :]
    nothing = jnp.zeros((1, width), F32)
    keys = product(context, nothing, nothing, attn_weight, width, False)

    rows = patches // CHUNKS

    def embedded(value):
        return [
            jnp.dot(
                value[i * rows : (i + 1) * rows], w_embed, preferred_element_type=F32
            ).astype(BF)
            for i in range(CHUNKS)
        ]

    hidden = embedded(latents[0])
    for turn in range(STEPS * BLOCKS):
        step, block = divmod(turn, BLOCKS)
        shift = modulation[step : step + 1, :width]
        scale = modulation[step : step + 1, width : 2 * width]
        gate = modulation[step : step + 1, 2 * width :]
        projected = [product(part, shift, scale, attn_weight, 0, True) for part in hidden]
        following = []
        for i in range(0, CHUNKS, TOGETHER):
            queries = tuple(range(i, i + TOGETHER))
            if following:
                bound, following = lax.optimization_barrier((gate, following))
            else:
                bound = gate
            following = following + list(
                attention(projected, keys, bias, bound, proj_weight, hidden, queries)
            )
        hidden = following
        if block < BLOCKS - 1:
            hidden = [hop(part, block, block + 1) for part in hidden]
        else:
            final = jnp.concatenate(hidden, 0)
            velocity = jnp.dot(
                layer_norm(final).astype(BF), w_final, preferred_element_type=F32
            )
            latent = latent + (levels[step + 1] - levels[step]) / 1000.0 * velocity
            if step < STEPS - 1:
                hidden = embedded(hop(latent.astype(BF), block, 0))

    last = BLOCKS - 1
    latent = latent.reshape(patches * latent_width // 128, 128)
    moved = move(latent, [((last, b, 0, d), (m, b, 0, d)) for m, b, d in homes() if m != last])
    latent = jnp.where(x == last, latent, moved)
    spread = lax.all_to_all(
        latent.reshape(Z * Y, rows_here * latent_width // 128, 128),
        ("z", "y"),
        split_axis=0,
        concat_axis=0,
        tiled=True,
    )
    mine = lax.dynamic_index_in_dim(spread, (2 * x + c) * Y, 0, keepdims=False)
    return mine.reshape(latent_noise.shape)


def solution(mesh):
    inner = Mesh(mesh.devices.reshape(X, Z, Y, C), AXES)
    seq = ("z", "y")
    placed = (
        P("x", "c", seq, None),
        P(None, "c", None, seq),
        P(None, "c"),
        P(),
        P(seq, None),
        P(),
        P("x", "c", None),
        P("x", "c", None),
        P("x", "c", None),
        P(),
    )
    return jax.shard_map(
        on_device,
        mesh=inner,
        in_specs=placed,
        out_specs=P("x", "c", seq, None),
        check_vma=False,
    )
```

```python
import functools
import math

import jax
import jax.numpy as jnp
from jax import lax
from jax.experimental import pallas as pl
from jax.experimental.pallas import tpu as pltpu
from jax.sharding import Mesh, PartitionSpec as P

HEADS = 16
HEAD = 96
STEPS = 2
BLOCKS = 4
X, Z, Y, C = 4, 8, 4, 2
AXES = ("x", "z", "y", "c")
BF = jnp.bfloat16
F32 = jnp.float32
VMEM = 20 * 1024 * 1024
SPAN = 768
CHUNKS = 4
TOGETHER = 2

epsilon = 1e-06


def time_features(noise_level, feature_count):
    half_count = feature_count // 2
    wave_frequency = jnp.exp(
        -math.log(10000.0) * jnp.arange(half_count, dtype=F32) / half_count
    )
    angles = noise_level * wave_frequency
    return jnp.concatenate([jnp.cos(angles), jnp.sin(angles)]).astype(BF)


def flat(x, z, y, c):
    return ((x * Z + z) * Y + y) * C + c


def move(value, pairs):
    return lax.ppermute(value, AXES, [(flat(*a), flat(*b)) for a, b in pairs])


def homes():
    return [(z // 2, z, z % 2) for z in range(Z)]


def whole():
    return pl.BlockSpec(memory_space=pltpu.VMEM)


def scalar():
    return pl.BlockSpec(memory_space=pltpu.SMEM)


def params():
    return pltpu.CompilerParams(vmem_limit_bytes=VMEM)


def joined_kernel(core_ref, own_ref, other_ref, *refs):
    out_ref, sems = refs[-2:]
    half = own_ref.shape[0]
    core = core_ref[0]
    copies = (
        pltpu.make_async_copy(
            own_ref, out_ref.at[pl.ds(pl.multiple_of(core * half, 16), half), :], sems.at[0]
        ),
        pltpu.make_async_copy(
            other_ref, out_ref.at[pl.ds(pl.multiple_of((1 - core) * half, 16), half), :], sems.at[1]
        ),
    )
    for copy in copies:
        copy.start()
    for copy in copies:
        copy.wait()


def joined(core, own, other, after):
    half, columns = own.shape
    return pl.pallas_call(
        joined_kernel,
        in_specs=[scalar()]
        + [pl.BlockSpec(memory_space=pltpu.HBM)] * 2
        + [pl.BlockSpec(memory_space=pl.ANY)] * len(after),
        out_specs=whole(),
        out_shape=jax.ShapeDtypeStruct((2 * half, columns), BF),
        scratch_shapes=[pltpu.SemaphoreType.DMA((2,))],
        compiler_params=params(),
        cost_estimate=pl.CostEstimate(
            flops=0, bytes_accessed=8 * half * columns, transcendentals=0
        ),
        name="joined",
    )(core, own, other, *after)


def normal(values):
    center = values - jnp.mean(values, axis=-1, keepdims=True)
    spread = jnp.mean(center * center, axis=-1, keepdims=True)
    return center * lax.rsqrt(spread + epsilon)


def product_kernel(*refs, pieces, column):
    row_refs, refs = refs[:pieces], refs[pieces:]
    weight_ref, refs = refs[0], refs[1:]
    out_ref, source = refs[-2:]
    done = 0
    for ref in row_refs:
        count = ref.shape[0]
        for i in range(0, count, 64):
            values = ref[i : i + 64, :]
            if column == 0:
                shift_ref, scale_ref = refs[:2]
                values = normal(values.astype(F32))
                values = (values * (1.0 + scale_ref[...]) + shift_ref[...]).astype(BF)
            source[done + i : done + i + 64, :] = values
        done += count
    for i in range(out_ref.shape[1] // SPAN):
        there = slice(i * SPAN, (i + 1) * SPAN)
        here = slice(column + i * SPAN, column + (i + 1) * SPAN)
        out_ref[:, there] = jnp.dot(
            source[...], weight_ref[:, here], preferred_element_type=F32
        ).astype(BF)


def product(rows, weight, column, modulate=(), after=()):
    count = sum(part.shape[0] for part in rows)
    width = weight.shape[0]
    columns = weight.shape[1] - column
    return pl.pallas_call(
        functools.partial(product_kernel, pieces=len(rows), column=column),
        in_specs=[whole()] * (len(rows) + 1 + len(modulate))
        + [pl.BlockSpec(memory_space=pl.ANY)] * len(after),
        out_specs=whole(),
        out_shape=jax.ShapeDtypeStruct((count, columns), BF),
        cost_estimate=pl.CostEstimate(
            flops=2 * count * width * columns,
            bytes_accessed=2 * 1024 * 1024,
            transcendentals=0,
        ),
        scratch_shapes=[pltpu.VMEM((count, width), BF)],
        compiler_params=params(),
        name="product",
    )(*rows, weight, *modulate, *after)


def embed_kernel(latent_ref, weight_ref, *out_refs):
    done = 0
    for ref in out_refs:
        count = ref.shape[0]
        ref[...] = jnp.dot(
            latent_ref[done : done + count, :], weight_ref[...], preferred_element_type=F32
        ).astype(BF)
        done += count


def embedded(latent, weight):
    rows = latent.shape[0] // CHUNKS
    return pl.pallas_call(
        embed_kernel,
        in_specs=[whole()] * 2,
        out_specs=[whole()] * CHUNKS,
        out_shape=[jax.ShapeDtypeStruct((rows, weight.shape[1]), BF)] * CHUNKS,
        compiler_params=params(),
        name="embed",
    )(latent, weight)


def finish_kernel(pace_ref, *refs, step):
    *row_refs, weight_ref, latent_ref, out_ref, rounded_ref = refs
    pace = pace_ref[step]
    done = 0
    for ref in row_refs:
        count = ref.shape[0]
        there = slice(done, done + count)
        velocity = jnp.dot(
            normal(ref[...].astype(F32)).astype(BF),
            weight_ref[...],
            preferred_element_type=F32,
        )
        latent = latent_ref[there, :] + pace * velocity
        out_ref[there, :] = latent
        rounded_ref[there, :] = latent.astype(BF)
        done += count


def finished(pace, hidden, weight, latent, step):
    return pl.pallas_call(
        functools.partial(finish_kernel, step=step),
        in_specs=[scalar()] + [whole()] * (len(hidden) + 2),
        out_specs=[whole()] * 2,
        out_shape=[
            jax.ShapeDtypeStruct(latent.shape, F32),
            jax.ShapeDtypeStruct(latent.shape, BF),
        ],
        compiler_params=params(),
        name="finish",
    )(pace, *hidden, weight, latent)


def spread_kernel(parts_ref, out_ref):
    count = out_ref.shape[1]
    total = parts_ref[0, :count].astype(F32)
    for k in range(1, parts_ref.shape[0]):
        total = total + parts_ref[k, :count].astype(F32)
    for k in range(out_ref.shape[0]):
        out_ref[k] = total.astype(BF)


def spread_over(parts, copies, count):
    return pl.pallas_call(
        spread_kernel,
        in_specs=[whole()],
        out_specs=whole(),
        out_shape=jax.ShapeDtypeStruct((copies, count, parts.shape[2]), BF),
        compiler_params=params(),
        name="spread",
    )(parts)


def twice_kernel(rows_ref, out_ref):
    for k in range(out_ref.shape[0]):
        out_ref[k] = rows_ref[k * rows_ref.shape[0] // out_ref.shape[0]]


def twice(rows, copies):
    return pl.pallas_call(
        twice_kernel,
        in_specs=[whole()],
        out_specs=whole(),
        out_shape=jax.ShapeDtypeStruct((copies,) + rows.shape[1:], BF),
        compiler_params=params(),
        name="twice",
    )(rows)


def attention_kernel(*refs, queries, blocks):
    projected, refs = refs[:blocks], refs[blocks:]
    text_ref, bias_ref, gate_ref, weight_ref, *refs = refs
    count = len(queries)
    hidden_refs, out_refs, attended = refs[:count], refs[-count - 1 : -1], refs[-1]
    inner = weight_ref.shape[0]
    factor = math.log2(math.e) / math.sqrt(HEAD)
    lanes = lax.broadcasted_iota(jnp.int32, (1, 128), 1)
    wide = lax.broadcasted_iota(jnp.int32, (1, 256), 1)
    bias = bias_ref[...]
    contract = (((1,), (1,)), ((), ()))

    def group(g, carry):
        base = pl.multiple_of(g * 4 * HEAD, 128)
        outs = []
        for h in range(4):
            low, high = h * HEAD, (h + 1) * HEAD
            start, stop = low // 128 * 128, -(-high // 128) * 128
            width = stop - start

            def window(refs, offset):
                there = pl.ds(pl.multiple_of(base + start + offset, 128), width)
                return jnp.concatenate([ref[:, there] for ref in refs], 0)

            index = lanes if width == 128 else wide
            mask = ((index >= low - start) & (index < high - start)).astype(F32).astype(BF)
            q = window([projected[i] for i in queries], 0) * mask
            image = lax.dot_general(
                q, window(projected, inner), contract, preferred_element_type=F32
            )
            text = lax.dot_general(
                q, window([text_ref], 0), contract, preferred_element_type=F32
            )
            text = text + bias
            top = jnp.maximum(
                jnp.max(image, axis=-1, keepdims=True), jnp.max(text, axis=-1, keepdims=True)
            )
            image = jnp.exp2((image - top) * factor)
            text = jnp.exp2((text - top) * factor)
            total = jnp.sum(image, axis=-1, keepdims=True) + jnp.sum(text, axis=-1, keepdims=True)
            value = jnp.dot(
                image.astype(BF), window(projected, 2 * inner), preferred_element_type=F32
            ) + jnp.dot(
                text.astype(BF), window([text_ref], inner), preferred_element_type=F32
            )
            outs.append(value * (1.0 / total))
        tiles = (
            jnp.where(lanes < 96, outs[0], outs[1][:, :128]),
            jnp.where(lanes < 64, outs[1][:, 128:], outs[2][:, :128]),
            jnp.where(lanes < 32, outs[2][:, 128:], outs[3]),
        )
        for j, tile in enumerate(tiles):
            attended[:, pl.ds(pl.multiple_of(base + j * 128, 128), 128)] = tile.astype(BF)
        return carry

    lax.fori_loop(0, inner // (4 * HEAD), group, 0)
    for i in range(weight_ref.shape[1] // SPAN):
        there = slice(i * SPAN, (i + 1) * SPAN)
        update = gate_ref[:, there] * jnp.dot(
            attended[...], weight_ref[:, there], preferred_element_type=F32
        )
        done = 0
        for hidden_ref, out_ref in zip(hidden_refs, out_refs):
            count = hidden_ref.shape[0]
            part = update[done : done + count]
            out_ref[:, there] = (hidden_ref[:, there].astype(F32) + part).astype(BF)
            done += count


def attention(projected, text, bias, gate, weight, hidden, queries, after=()):
    hidden = [hidden[i] for i in queries]
    rows = sum(part.shape[0] for part in hidden)
    return pl.pallas_call(
        functools.partial(attention_kernel, queries=queries, blocks=len(projected)),
        in_specs=[whole()] * (len(projected) + 4 + len(hidden))
        + [pl.BlockSpec(memory_space=pl.ANY)] * len(after),
        cost_estimate=pl.CostEstimate(
            flops=4 * rows * weight.shape[0] * weight.shape[1],
            bytes_accessed=8 * 1024 * 1024,
            transcendentals=0,
        ),
        out_specs=[whole()] * len(hidden),
        out_shape=[jax.ShapeDtypeStruct(part.shape, BF) for part in hidden],
        scratch_shapes=[pltpu.VMEM((rows, weight.shape[0]), BF)],
        compiler_params=params(),
        name="attention",
    )(*projected, text, bias, gate, weight, *hidden, *after)


def on_device(
    latent_noise,
    text_rows,
    text_lengths,
    plan,
    context_weight,
    w_embed,
    w_attention,
    w_project,
    w_modulate,
    w_final,
):
    x, z, y, c = (lax.axis_index(name) for name in AXES)
    width = w_embed.shape[1]
    latent_width = latent_noise.shape[3]
    rows_here = latent_noise.shape[2]
    patches = rows_here * Z * Y
    text_total = text_rows.shape[2]
    core = jnp.reshape(c, (1,)).astype(jnp.int32)
    image = z // 2

    def across(value):
        return move(
            value, [((a, b, 0, 1 - b % C), (a, b, 0, b % C)) for a in range(X) for b in range(Z)]
        )

    def hop(value, source, target):
        return move(value, [((source, b, 0, d), (target, b, 0, d)) for _, b, d in homes()])

    levels = plan.astype(F32)
    mod_rows = w_modulate.shape[1]
    features = jnp.stack([time_features(levels[k], C * mod_rows) for k in range(STEPS)])
    features = lax.dynamic_slice_in_dim(features, c * mod_rows, mod_rows, 1)
    modulation = jnp.dot(features, w_modulate[0], preferred_element_type=F32)
    modulation = modulation + across(modulation)

    text = lax.dynamic_index_in_dim(text_rows[:, 0], x, 0, keepdims=False)
    partial = jnp.dot(text, context_weight, preferred_element_type=F32).astype(BF)
    attn_mine, proj_mine, partial = lax.optimization_barrier(
        (w_attention[0], w_project[0], partial)
    )
    quarter = text_total // Y
    eighth = quarter // Z
    latent = latent_noise[0, 0].reshape(1, rows_here * latent_width)
    high = latent.astype(BF)
    low = (latent - high.astype(F32)).astype(BF)
    both = jnp.pad(jnp.concatenate([high, low], 0), ((0, 0), (0, width - latent.shape[1])))
    parts = lax.all_to_all(
        jnp.concatenate(
            [partial.reshape(Y, quarter, width), jnp.broadcast_to(both[None], (Y, 2, width))], 1
        ),
        "y",
        split_axis=0,
        concat_axis=0,
        tiled=True,
    )
    summed = jnp.sum(parts[:, :quarter].astype(F32), axis=0).astype(BF)
    both = parts[:, quarter:].reshape(1, 2 * Y, width)
    parts = lax.all_to_all(
        jnp.concatenate(
            [summed.reshape(Z, eighth, width), jnp.broadcast_to(both, (Z, 2 * Y, width))], 1
        ),
        "z",
        split_axis=0,
        concat_axis=0,
        tiled=True,
    )
    both = parts[:, eighth:].reshape(patches // rows_here, 2, width)[:, :, : latent.shape[1]]
    both = jnp.transpose(both, (1, 0, 2)).reshape(2, patches * latent_width // 128, 128)

    def to_plane(value, plane):
        sent = move(value, [((m, b, 0, d), (plane, b, 0, d)) for m, b, d in homes() if m != plane])
        return jnp.where(image == plane, value, sent)

    first = to_plane(both[0], 0).reshape(patches, latent_width)
    latent = to_plane(both, BLOCKS - 1)
    latent = (latent[0].astype(F32) + latent[1].astype(F32)).reshape(patches, latent_width)
    length = jnp.sum(jnp.where(jnp.arange(X) == image, text_lengths[:, 0], 0))
    bias = jnp.where(jnp.arange(text_total) < length, 0.0, -1e30).astype(F32)[None, :]
    pace = (levels[1:] - levels[:-1]) / 1000.0
    shifts, scales, gates = (
        [modulation[k : k + 1, part * width : (part + 1) * width] for k in range(STEPS)]
        for part in range(3)
    )

    ready = (first, latent, bias, *shifts, *scales, *gates)
    attn_weight = joined(core, attn_mine, across(attn_mine), ready)
    proj_weight = joined(core, proj_mine, across(proj_mine), (attn_weight,))

    shared = lax.all_to_all(
        spread_over(parts, X, eighth), "x", split_axis=0, concat_axis=0, tiled=True
    )
    shared = lax.all_to_all(twice(shared, Z), "z", split_axis=0, concat_axis=0, tiled=True)
    pieces = [shared.reshape(quarter, width)]
    for k in range(1, Y):
        pieces.append(
            move(
                pieces[0],
                [((a, b, k, b % C), (a, b, 0, b % C)) for a in range(X) for b in range(Z)],
            )
        )
    keys = product(pieces, attn_weight, width)

    hidden = embedded(first, w_embed)
    for turn in range(STEPS * BLOCKS):
        step, block = divmod(turn, BLOCKS)
        gate = gates[step]
        projected = []
        for part in hidden:
            projected.append(
                product(
                    [part], attn_weight, 0, (shifts[step], scales[step]), tuple(projected[-1:])
                )
            )
        following = []
        for i in range(0, CHUNKS, TOGETHER):
            queries = tuple(range(i, i + TOGETHER))
            following = following + list(
                attention(
                    projected,
                    keys,
                    bias,
                    gate,
                    proj_weight,
                    hidden,
                    queries,
                    tuple(following[-1:]),
                )
            )
        hidden = following
        if block < BLOCKS - 1:
            hidden = [hop(part, block, block + 1) for part in hidden]
        else:
            latent, rounded = finished(pace, hidden, w_final, latent, step)
            if step < STEPS - 1:
                hidden = embedded(hop(rounded, block, 0), w_embed)

    last = BLOCKS - 1
    latent = latent.reshape(patches * latent_width // 128, 128)
    moved = move(latent, [((last, b, 0, d), (m, b, 0, d)) for m, b, d in homes() if m != last])
    latent = jnp.where(x == last, latent, moved)
    spread = lax.all_to_all(
        latent.reshape(Z * Y, rows_here * latent_width // 128, 128),
        ("z", "y"),
        split_axis=0,
        concat_axis=0,
        tiled=True,
    )
    mine = lax.dynamic_index_in_dim(spread, (2 * x + c) * Y, 0, keepdims=False)
    return mine.reshape(latent_noise.shape)


def solution(mesh):
    inner = Mesh(mesh.devices.reshape(X, Z, Y, C), AXES)
    seq = ("z", "y")
    placed = (
        P("x", "c", seq, None),
        P(None, "c", None, seq),
        P(None, "c"),
        P(),
        P(seq, None),
        P(),
        P("x", "c", None),
        P("x", "c", None),
        P("x", "c", None),
        P(),
    )
    return jax.shard_map(
        on_device,
        mesh=inner,
        in_specs=placed,
        out_specs=P("x", "c", seq, None),
        check_vma=False,
    )
```

```python
import functools
import math

import jax
import jax.numpy as jnp
from jax import lax
from jax.experimental import pallas as pl
from jax.experimental.pallas import tpu as pltpu
from jax.sharding import Mesh, PartitionSpec as P

HEADS = 16
HEAD = 96
STEPS = 2
BLOCKS = 4
X, Z, Y, C = 4, 8, 4, 2
AXES = ("x", "z", "y", "c")
BF = jnp.bfloat16
F32 = jnp.float32
VMEM = 20 * 1024 * 1024
SPAN = 768
CHUNKS = 4
TOGETHER = 2

epsilon = 1e-06


def time_features(noise_level, feature_count):
    half_count = feature_count // 2
    wave_frequency = jnp.exp(
        -math.log(10000.0) * jnp.arange(half_count, dtype=F32) / half_count
    )
    angles = noise_level * wave_frequency
    return jnp.concatenate([jnp.cos(angles), jnp.sin(angles)]).astype(BF)


def flat(x, z, y, c):
    return ((x * Z + z) * Y + y) * C + c


def move(value, pairs):
    return lax.ppermute(value, AXES, [(flat(*a), flat(*b)) for a, b in pairs])


def homes():
    return [(z // 2, z, z % 2) for z in range(Z)]


def whole():
    return pl.BlockSpec(memory_space=pltpu.VMEM)


def scalar():
    return pl.BlockSpec(memory_space=pltpu.SMEM)


def params():
    return pltpu.CompilerParams(vmem_limit_bytes=VMEM)


def joined_kernel(core_ref, own_ref, *refs, pieces):
    piece_refs, (out_ref, sems) = refs[:pieces], refs[-2:]
    half = own_ref.shape[0]
    core = core_ref[0]

    def target(start, count):
        return out_ref.at[pl.ds(pl.multiple_of(start, 16), count), :]

    copies = [pltpu.make_async_copy(own_ref, target(core * half, half), sems.at[0])]
    done = 0
    for k, ref in enumerate(piece_refs):
        count = ref.shape[0]
        copies.append(
            pltpu.make_async_copy(ref, target((1 - core) * half + done, count), sems.at[k + 1])
        )
        done += count
    for copy in copies:
        copy.start()
    for copy in copies:
        copy.wait()


def joined(core, own, pieces, after):
    half, columns = own.shape
    return pl.pallas_call(
        functools.partial(joined_kernel, pieces=len(pieces)),
        in_specs=[scalar()]
        + [pl.BlockSpec(memory_space=pltpu.HBM)] * (1 + len(pieces))
        + [pl.BlockSpec(memory_space=pl.ANY)] * len(after),
        out_specs=whole(),
        out_shape=jax.ShapeDtypeStruct((2 * half, columns), BF),
        scratch_shapes=[pltpu.SemaphoreType.DMA((1 + len(pieces),))],
        compiler_params=params(),
        cost_estimate=pl.CostEstimate(flops=0, bytes_accessed=1024, transcendentals=0),
        name="joined",
    )(core, own, *pieces, *after)


def normal(values):
    center = values - jnp.mean(values, axis=-1, keepdims=True)
    spread = jnp.mean(center * center, axis=-1, keepdims=True)
    return center * lax.rsqrt(spread + epsilon)


def product_kernel(*refs, pieces, column):
    row_refs, refs = refs[:pieces], refs[pieces:]
    weight_ref, refs = refs[0], refs[1:]
    out_ref, source = refs[-2:]
    done = 0
    for ref in row_refs:
        count = ref.shape[0]
        for i in range(0, count, 64):
            values = ref[i : i + 64, :]
            if column == 0:
                shift_ref, scale_ref = refs[:2]
                values = normal(values.astype(F32))
                values = (values * (1.0 + scale_ref[...]) + shift_ref[...]).astype(BF)
            source[done + i : done + i + 64, :] = values
        done += count
    for i in range(out_ref.shape[1] // SPAN):
        there = slice(i * SPAN, (i + 1) * SPAN)
        here = slice(column + i * SPAN, column + (i + 1) * SPAN)
        out_ref[:, there] = jnp.dot(
            source[...], weight_ref[:, here], preferred_element_type=F32
        ).astype(BF)


def product(rows, weight, column, modulate=(), after=()):
    count = sum(part.shape[0] for part in rows)
    width = weight.shape[0]
    columns = weight.shape[1] - column
    return pl.pallas_call(
        functools.partial(product_kernel, pieces=len(rows), column=column),
        in_specs=[whole()] * (len(rows) + 1 + len(modulate))
        + [pl.BlockSpec(memory_space=pl.ANY)] * len(after),
        out_specs=whole(),
        out_shape=jax.ShapeDtypeStruct((count, columns), BF),
        cost_estimate=pl.CostEstimate(
            flops=2 * count * width * columns,
            bytes_accessed=2 * 1024 * 1024,
            transcendentals=0,
        ),
        scratch_shapes=[pltpu.VMEM((count, width), BF)],
        compiler_params=params(),
        name="product",
    )(*rows, weight, *modulate, *after)


def embed_kernel(latent_ref, weight_ref, *out_refs):
    done = 0
    for ref in out_refs:
        count = ref.shape[0]
        ref[...] = jnp.dot(
            latent_ref[done : done + count, :], weight_ref[...], preferred_element_type=F32
        ).astype(BF)
        done += count


def embedded(latent, weight):
    rows = latent.shape[0] // CHUNKS
    return pl.pallas_call(
        embed_kernel,
        in_specs=[whole()] * 2,
        out_specs=[whole()] * CHUNKS,
        out_shape=[jax.ShapeDtypeStruct((rows, weight.shape[1]), BF)] * CHUNKS,
        compiler_params=params(),
        name="embed",
    )(latent, weight)


def finish_kernel(pace_ref, *refs, step):
    *row_refs, weight_ref, latent_ref, out_ref, rounded_ref = refs
    pace = pace_ref[step]
    done = 0
    for ref in row_refs:
        count = ref.shape[0]
        there = slice(done, done + count)
        velocity = jnp.dot(
            normal(ref[...].astype(F32)).astype(BF),
            weight_ref[...],
            preferred_element_type=F32,
        )
        latent = latent_ref[there, :] + pace * velocity
        out_ref[there, :] = latent
        rounded_ref[there, :] = latent.astype(BF)
        done += count


def finished(pace, hidden, weight, latent, step):
    return pl.pallas_call(
        functools.partial(finish_kernel, step=step),
        in_specs=[scalar()] + [whole()] * (len(hidden) + 2),
        out_specs=[whole()] * 2,
        out_shape=[
            jax.ShapeDtypeStruct(latent.shape, F32),
            jax.ShapeDtypeStruct(latent.shape, BF),
        ],
        compiler_params=params(),
        name="finish",
    )(pace, *hidden, weight, latent)


def spread_kernel(parts_ref, out_ref):
    count = out_ref.shape[1]
    total = parts_ref[0, :count].astype(F32)
    for k in range(1, parts_ref.shape[0]):
        total = total + parts_ref[k, :count].astype(F32)
    for k in range(out_ref.shape[0]):
        out_ref[k] = total.astype(BF)


def spread_over(parts, copies, count):
    return pl.pallas_call(
        spread_kernel,
        in_specs=[whole()],
        out_specs=whole(),
        out_shape=jax.ShapeDtypeStruct((copies, count, parts.shape[2]), BF),
        compiler_params=params(),
        name="spread",
    )(parts)


def twice_kernel(rows_ref, *refs):
    out_ref = refs[-1]
    for k in range(out_ref.shape[0]):
        out_ref[k] = rows_ref[k * rows_ref.shape[0] // out_ref.shape[0]]


def twice(rows, copies, after):
    return pl.pallas_call(
        twice_kernel,
        in_specs=[whole()] + [pl.BlockSpec(memory_space=pl.ANY)] * len(after),
        out_specs=whole(),
        out_shape=jax.ShapeDtypeStruct((copies,) + rows.shape[1:], BF),
        compiler_params=params(),
        name="twice",
    )(rows, *after)


def attention_kernel(*refs, queries, blocks):
    projected, refs = refs[:blocks], refs[blocks:]
    text_ref, bias_ref, gate_ref, weight_ref, *refs = refs
    count = len(queries)
    hidden_refs, out_refs, attended = refs[:count], refs[-count - 1 : -1], refs[-1]
    inner = weight_ref.shape[0]
    factor = math.log2(math.e) / math.sqrt(HEAD)
    lanes = lax.broadcasted_iota(jnp.int32, (1, 128), 1)
    wide = lax.broadcasted_iota(jnp.int32, (1, 256), 1)
    bias = bias_ref[...]
    contract = (((1,), (1,)), ((), ()))

    def group(g, carry):
        base = pl.multiple_of(g * 4 * HEAD, 128)
        outs = []
        for h in range(4):
            low, high = h * HEAD, (h + 1) * HEAD
            start, stop = low // 128 * 128, -(-high // 128) * 128
            width = stop - start

            def window(refs, offset):
                there = pl.ds(pl.multiple_of(base + start + offset, 128), width)
                return jnp.concatenate([ref[:, there] for ref in refs], 0)

            index = lanes if width == 128 else wide
            mask = ((index >= low - start) & (index < high - start)).astype(F32).astype(BF)
            q = window([projected[i] for i in queries], 0) * mask
            image = lax.dot_general(
                q, window(projected, inner), contract, preferred_element_type=F32
            )
            text = lax.dot_general(
                q, window([text_ref], 0), contract, preferred_element_type=F32
            )
            text = text + bias
            top = jnp.maximum(
                jnp.max(image, axis=-1, keepdims=True), jnp.max(text, axis=-1, keepdims=True)
            )
            image = jnp.exp2((image - top) * factor)
            text = jnp.exp2((text - top) * factor)
            total = jnp.sum(image, axis=-1, keepdims=True) + jnp.sum(text, axis=-1, keepdims=True)
            value = jnp.dot(
                image.astype(BF), window(projected, 2 * inner), preferred_element_type=F32
            ) + jnp.dot(
                text.astype(BF), window([text_ref], inner), preferred_element_type=F32
            )
            outs.append(value * (1.0 / total))
        tiles = (
            jnp.where(lanes < 96, outs[0], outs[1][:, :128]),
            jnp.where(lanes < 64, outs[1][:, 128:], outs[2][:, :128]),
            jnp.where(lanes < 32, outs[2][:, 128:], outs[3]),
        )
        for j, tile in enumerate(tiles):
            attended[:, pl.ds(pl.multiple_of(base + j * 128, 128), 128)] = tile.astype(BF)
        return carry

    lax.fori_loop(0, inner // (4 * HEAD), group, 0)
    for i in range(weight_ref.shape[1] // SPAN):
        there = slice(i * SPAN, (i + 1) * SPAN)
        update = gate_ref[:, there] * jnp.dot(
            attended[...], weight_ref[:, there], preferred_element_type=F32
        )
        done = 0
        for hidden_ref, out_ref in zip(hidden_refs, out_refs):
            count = hidden_ref.shape[0]
            part = update[done : done + count]
            out_ref[:, there] = (hidden_ref[:, there].astype(F32) + part).astype(BF)
            done += count


def attention(projected, text, bias, gate, weight, hidden, queries, after=()):
    hidden = [hidden[i] for i in queries]
    rows = sum(part.shape[0] for part in hidden)
    return pl.pallas_call(
        functools.partial(attention_kernel, queries=queries, blocks=len(projected)),
        in_specs=[whole()] * (len(projected) + 4 + len(hidden))
        + [pl.BlockSpec(memory_space=pl.ANY)] * len(after),
        cost_estimate=pl.CostEstimate(
            flops=4 * rows * weight.shape[0] * weight.shape[1],
            bytes_accessed=8 * 1024 * 1024,
            transcendentals=0,
        ),
        out_specs=[whole()] * len(hidden),
        out_shape=[jax.ShapeDtypeStruct(part.shape, BF) for part in hidden],
        scratch_shapes=[pltpu.VMEM((rows, weight.shape[0]), BF)],
        compiler_params=params(),
        name="attention",
    )(*projected, text, bias, gate, weight, *hidden, *after)


def on_device(
    latent_noise,
    text_rows,
    text_lengths,
    plan,
    context_weight,
    w_embed,
    w_attention,
    w_project,
    w_modulate,
    w_final,
):
    x, z, y, c = (lax.axis_index(name) for name in AXES)
    width = w_embed.shape[1]
    latent_width = latent_noise.shape[3]
    rows_here = latent_noise.shape[2]
    patches = rows_here * Z * Y
    text_total = text_rows.shape[2]
    core = jnp.reshape(c, (1,)).astype(jnp.int32)
    image = z // 2

    def across(value):
        return move(
            value, [((a, b, 0, 1 - b % C), (a, b, 0, b % C)) for a in range(X) for b in range(Z)]
        )

    def hop(value, source, target):
        return move(value, [((source, b, 0, d), (target, b, 0, d)) for _, b, d in homes()])

    levels = plan.astype(F32)
    mod_rows = w_modulate.shape[1]
    features = jnp.stack([time_features(levels[k], C * mod_rows) for k in range(STEPS)])
    features = lax.dynamic_slice_in_dim(features, c * mod_rows, mod_rows, 1)
    modulation = jnp.dot(features, w_modulate[0], preferred_element_type=F32)
    modulation = modulation + across(modulation)

    text = lax.dynamic_index_in_dim(text_rows[:, 0], x, 0, keepdims=False)
    partial = jnp.dot(text, context_weight, preferred_element_type=F32).astype(BF)
    attn_mine, proj_mine = w_attention[0], w_project[0]
    third = attn_mine.shape[0] // 3

    def beside(operand, piece):
        operand, piece = lax.optimization_barrier((operand, piece))
        return operand, across(piece)

    quarter = text_total // Y
    eighth = quarter // Z
    latent = latent_noise[0, 0].reshape(1, rows_here * latent_width)
    high = latent.astype(BF)
    low = (latent - high.astype(F32)).astype(BF)
    both = jnp.pad(jnp.concatenate([high, low], 0), ((0, 0), (0, width - latent.shape[1])))
    message = jnp.concatenate(
        [partial.reshape(Y, quarter, width), jnp.broadcast_to(both[None], (Y, 2, width))], 1
    )
    message, piece = beside(message, attn_mine[:third])
    attn_pieces = [piece]
    parts = lax.all_to_all(message, "y", split_axis=0, concat_axis=0, tiled=True)
    summed = jnp.sum(parts[:, :quarter].astype(F32), axis=0).astype(BF)
    both = parts[:, quarter:].reshape(1, 2 * Y, width)
    message = jnp.concatenate(
        [summed.reshape(Z, eighth, width), jnp.broadcast_to(both, (Z, 2 * Y, width))], 1
    )
    message, piece = beside(message, attn_mine[third : 2 * third])
    attn_pieces.append(piece)
    parts = lax.all_to_all(message, "z", split_axis=0, concat_axis=0, tiled=True)
    both = parts[:, eighth:].reshape(patches // rows_here, 2, width)[:, :, : latent.shape[1]]
    both = jnp.transpose(both, (1, 0, 2)).reshape(2, patches * latent_width // 128, 128)

    def to_plane(value, plane):
        sent = move(value, [((m, b, 0, d), (plane, b, 0, d)) for m, b, d in homes() if m != plane])
        return jnp.where(image == plane, value, sent)

    first = to_plane(both[0], 0).reshape(patches, latent_width)
    latent = to_plane(both, BLOCKS - 1)
    latent = (latent[0].astype(F32) + latent[1].astype(F32)).reshape(patches, latent_width)
    length = jnp.sum(jnp.where(jnp.arange(X) == image, text_lengths[:, 0], 0))
    bias = jnp.where(jnp.arange(text_total) < length, 0.0, -1e30).astype(F32)[None, :]
    pace = (levels[1:] - levels[:-1]) / 1000.0
    shifts, scales, gates = (
        [modulation[k : k + 1, part * width : (part + 1) * width] for k in range(STEPS)]
        for part in range(3)
    )

    message, piece = beside(spread_over(parts, X, eighth), attn_mine[2 * third :])
    attn_pieces.append(piece)
    shared = lax.all_to_all(message, "x", split_axis=0, concat_axis=0, tiled=True)
    early = (first, latent, bias, w_final, w_embed, *shifts, *scales, *gates)
    message, piece = beside(twice(shared, Z, early), proj_mine)
    shared = lax.all_to_all(message, "z", split_axis=0, concat_axis=0, tiled=True)
    ready = (first, latent, bias, w_final, w_embed, *shifts, *scales, *gates)
    attn_weight = joined(core, attn_mine, attn_pieces, ready)
    hidden = embedded(first, w_embed)

    def products(hidden, step):
        done = []
        for part in hidden:
            done.append(
                product([part], attn_weight, 0, (shifts[step], scales[step]), tuple(done[-1:]))
            )
        return done

    projected = products(hidden, 0)
    pieces = [shared.reshape(quarter, width)]
    for k in range(1, Y):
        pieces.append(
            move(
                pieces[0],
                [((a, b, k, b % C), (a, b, 0, b % C)) for a in range(X) for b in range(Z)],
            )
        )
    proj_weight = joined(core, proj_mine, [piece], ready)
    keys = product(pieces, attn_weight, width)

    for turn in range(STEPS * BLOCKS):
        step, block = divmod(turn, BLOCKS)
        gate = gates[step]
        if turn > 0:
            projected = products(hidden, step)
        following = []
        for i in range(0, CHUNKS, TOGETHER):
            queries = tuple(range(i, i + TOGETHER))
            following = following + list(
                attention(
                    projected,
                    keys,
                    bias,
                    gate,
                    proj_weight,
                    hidden,
                    queries,
                    tuple(following[-1:]),
                )
            )
        hidden = following
        if block < BLOCKS - 1:
            hidden = [hop(part, block, block + 1) for part in hidden]
        else:
            latent, rounded = finished(pace, hidden, w_final, latent, step)
            if step < STEPS - 1:
                hidden = embedded(hop(rounded, block, 0), w_embed)

    last = BLOCKS - 1
    latent = latent.reshape(patches * latent_width // 128, 128)
    moved = move(latent, [((last, b, 0, d), (m, b, 0, d)) for m, b, d in homes() if m != last])
    latent = jnp.where(x == last, latent, moved)
    spread = lax.all_to_all(
        latent.reshape(Z * Y, rows_here * latent_width // 128, 128),
        ("z", "y"),
        split_axis=0,
        concat_axis=0,
        tiled=True,
    )
    mine = lax.dynamic_index_in_dim(spread, (2 * x + c) * Y, 0, keepdims=False)
    return mine.reshape(latent_noise.shape)


def solution(mesh):
    inner = Mesh(mesh.devices.reshape(X, Z, Y, C), AXES)
    seq = ("z", "y")
    placed = (
        P("x", "c", seq, None),
        P(None, "c", None, seq),
        P(None, "c"),
        P(),
        P(seq, None),
        P(),
        P("x", "c", None),
        P("x", "c", None),
        P("x", "c", None),
        P(),
    )
    return jax.shard_map(
        on_device,
        mesh=inner,
        in_specs=placed,
        out_specs=P("x", "c", seq, None),
        check_vma=False,
    )
```

```python
import functools
import math

import jax
import jax.numpy as jnp
from jax import lax
from jax.experimental import pallas as pl
from jax.experimental.pallas import tpu as pltpu
from jax.sharding import Mesh, PartitionSpec as P

HEADS = 16
HEAD = 96
STEPS = 2
BLOCKS = 4
X, Z, Y, C = 4, 8, 4, 2
AXES = ("x", "z", "y", "c")
BF = jnp.bfloat16
F32 = jnp.float32
VMEM = 20 * 1024 * 1024
SPAN = 768
CALLS = ((128, 128), (128, 128))
CHUNKS = sum(CALLS, ())

epsilon = 1e-06


def time_features(noise_level, feature_count):
    half_count = feature_count // 2
    wave_frequency = jnp.exp(
        -math.log(10000.0) * jnp.arange(half_count, dtype=F32) / half_count
    )
    angles = noise_level * wave_frequency
    return jnp.concatenate([jnp.cos(angles), jnp.sin(angles)]).astype(BF)


def flat(x, z, y, c):
    return ((x * Z + z) * Y + y) * C + c


def move(value, pairs):
    return lax.ppermute(value, AXES, [(flat(*a), flat(*b)) for a, b in pairs])


def homes():
    return [(z // 2, z, z % 2) for z in range(Z)]


def whole():
    return pl.BlockSpec(memory_space=pltpu.VMEM)


def scalar():
    return pl.BlockSpec(memory_space=pltpu.SMEM)


def params():
    return pltpu.CompilerParams(vmem_limit_bytes=VMEM)


def joined_kernel(core_ref, own_ref, *refs, pieces):
    piece_refs, (out_ref, sems) = refs[:pieces], refs[-2:]
    half = own_ref.shape[0]
    core = core_ref[0]

    def target(start, count):
        return out_ref.at[pl.ds(pl.multiple_of(start, 16), count), :]

    copies = [pltpu.make_async_copy(own_ref, target(core * half, half), sems.at[0])]
    done = 0
    for k, ref in enumerate(piece_refs):
        count = ref.shape[0]
        copies.append(
            pltpu.make_async_copy(ref, target((1 - core) * half + done, count), sems.at[k + 1])
        )
        done += count
    for copy in copies:
        copy.start()
    for copy in copies:
        copy.wait()


def joined(core, own, pieces, after):
    half, columns = own.shape
    return pl.pallas_call(
        functools.partial(joined_kernel, pieces=len(pieces)),
        in_specs=[scalar()]
        + [pl.BlockSpec(memory_space=pltpu.HBM)] * (1 + len(pieces))
        + [pl.BlockSpec(memory_space=pl.ANY)] * len(after),
        out_specs=whole(),
        out_shape=jax.ShapeDtypeStruct((2 * half, columns), BF),
        scratch_shapes=[pltpu.SemaphoreType.DMA((1 + len(pieces),))],
        compiler_params=params(),
        cost_estimate=pl.CostEstimate(flops=0, bytes_accessed=1024, transcendentals=0),
        name="joined",
    )(core, own, *pieces, *after)


def normal(values):
    center = values - jnp.mean(values, axis=-1, keepdims=True)
    spread = jnp.mean(center * center, axis=-1, keepdims=True)
    return center * lax.rsqrt(spread + epsilon)


def product_kernel(*refs, pieces, column):
    row_refs, refs = refs[:pieces], refs[pieces:]
    weight_ref, refs = refs[0], refs[1:]
    out_ref, source = refs[-2:]
    done = 0
    for ref in row_refs:
        count = ref.shape[0]
        for i in range(0, count, 64):
            values = ref[i : i + 64, :]
            if column == 0:
                shift_ref, scale_ref = refs[:2]
                values = normal(values.astype(F32))
                values = (values * (1.0 + scale_ref[...]) + shift_ref[...]).astype(BF)
            source[done + i : done + i + 64, :] = values
        done += count
    for i in range(out_ref.shape[1] // SPAN):
        there = slice(i * SPAN, (i + 1) * SPAN)
        here = slice(column + i * SPAN, column + (i + 1) * SPAN)
        out_ref[:, there] = jnp.dot(
            source[...], weight_ref[:, here], preferred_element_type=F32
        ).astype(BF)


def product(rows, weight, column, modulate=(), after=()):
    count = sum(part.shape[0] for part in rows)
    width = weight.shape[0]
    columns = weight.shape[1] - column
    return pl.pallas_call(
        functools.partial(product_kernel, pieces=len(rows), column=column),
        in_specs=[whole()] * (len(rows) + 1 + len(modulate))
        + [pl.BlockSpec(memory_space=pl.ANY)] * len(after),
        out_specs=whole(),
        out_shape=jax.ShapeDtypeStruct((count, columns), BF),
        cost_estimate=pl.CostEstimate(
            flops=2 * count * width * columns,
            bytes_accessed=2 * 1024 * 1024,
            transcendentals=0,
        ),
        scratch_shapes=[pltpu.VMEM((count, width), BF)],
        compiler_params=params(),
        name="product",
    )(*rows, weight, *modulate, *after)


def embed_kernel(latent_ref, weight_ref, *out_refs):
    done = 0
    for ref in out_refs:
        count = ref.shape[0]
        ref[...] = jnp.dot(
            latent_ref[done : done + count, :], weight_ref[...], preferred_element_type=F32
        ).astype(BF)
        done += count


def embedded(latent, weight):
    return pl.pallas_call(
        embed_kernel,
        in_specs=[whole()] * 2,
        out_specs=[whole()] * len(CHUNKS),
        out_shape=[jax.ShapeDtypeStruct((rows, weight.shape[1]), BF) for rows in CHUNKS],
        compiler_params=params(),
        name="embed",
    )(latent, weight)


def finish_kernel(pace_ref, *refs, step):
    *row_refs, weight_ref, latent_ref, out_ref, rounded_ref = refs
    pace = pace_ref[step]
    done = 0
    for ref in row_refs:
        count = ref.shape[0]
        there = slice(done, done + count)
        velocity = jnp.dot(
            normal(ref[...].astype(F32)).astype(BF),
            weight_ref[...],
            preferred_element_type=F32,
        )
        latent = latent_ref[there, :] + pace * velocity
        out_ref[there, :] = latent
        rounded_ref[there, :] = latent.astype(BF)
        done += count


def finished(pace, hidden, weight, latent, step):
    return pl.pallas_call(
        functools.partial(finish_kernel, step=step),
        in_specs=[scalar()] + [whole()] * (len(hidden) + 2),
        out_specs=[whole()] * 2,
        out_shape=[
            jax.ShapeDtypeStruct(latent.shape, F32),
            jax.ShapeDtypeStruct(latent.shape, BF),
        ],
        compiler_params=params(),
        name="finish",
    )(pace, *hidden, weight, latent)


def spread_kernel(parts_ref, out_ref):
    count = out_ref.shape[1]
    total = parts_ref[0, :count].astype(F32)
    for k in range(1, parts_ref.shape[0]):
        total = total + parts_ref[k, :count].astype(F32)
    for k in range(out_ref.shape[0]):
        out_ref[k] = total.astype(BF)


def spread_over(parts, copies, count):
    return pl.pallas_call(
        spread_kernel,
        in_specs=[whole()],
        out_specs=whole(),
        out_shape=jax.ShapeDtypeStruct((copies, count, parts.shape[2]), BF),
        compiler_params=params(),
        name="spread",
    )(parts)


def twice_kernel(rows_ref, *refs):
    out_ref = refs[-1]
    for k in range(out_ref.shape[0]):
        out_ref[k] = rows_ref[k * rows_ref.shape[0] // out_ref.shape[0]]


def twice(rows, copies, after):
    return pl.pallas_call(
        twice_kernel,
        in_specs=[whole()] + [pl.BlockSpec(memory_space=pl.ANY)] * len(after),
        out_specs=whole(),
        out_shape=jax.ShapeDtypeStruct((copies,) + rows.shape[1:], BF),
        compiler_params=params(),
        name="twice",
    )(rows, *after)


def attention_kernel(*refs, queries, blocks):
    projected, refs = refs[:blocks], refs[blocks:]
    text_ref, bias_ref, gate_ref, weight_ref, *refs = refs
    count = len(queries)
    hidden_refs, out_refs, attended = refs[:count], refs[-count - 1 : -1], refs[-1]
    inner = weight_ref.shape[0]
    factor = math.log2(math.e) / math.sqrt(HEAD)
    lanes = lax.broadcasted_iota(jnp.int32, (1, 128), 1)
    wide = lax.broadcasted_iota(jnp.int32, (1, 256), 1)
    bias = bias_ref[...]
    contract = (((1,), (1,)), ((), ()))

    def group(g, carry):
        base = pl.multiple_of(g * 4 * HEAD, 128)
        outs = []
        for h in range(4):
            low, high = h * HEAD, (h + 1) * HEAD
            start, stop = low // 128 * 128, -(-high // 128) * 128
            width = stop - start

            def window(refs, offset):
                there = pl.ds(pl.multiple_of(base + start + offset, 128), width)
                return jnp.concatenate([ref[:, there] for ref in refs], 0)

            index = lanes if width == 128 else wide
            mask = ((index >= low - start) & (index < high - start)).astype(F32).astype(BF)
            q = window([projected[i] for i in queries], 0) * mask
            image = lax.dot_general(
                q, window(projected, inner), contract, preferred_element_type=F32
            )
            text = lax.dot_general(
                q, window([text_ref], 0), contract, preferred_element_type=F32
            )
            text = text + bias
            top = jnp.maximum(
                jnp.max(image, axis=-1, keepdims=True), jnp.max(text, axis=-1, keepdims=True)
            )
            image = jnp.exp2((image - top) * factor)
            text = jnp.exp2((text - top) * factor)
            total = jnp.sum(image, axis=-1, keepdims=True) + jnp.sum(text, axis=-1, keepdims=True)
            value = jnp.dot(
                image.astype(BF), window(projected, 2 * inner), preferred_element_type=F32
            ) + jnp.dot(
                text.astype(BF), window([text_ref], inner), preferred_element_type=F32
            )
            outs.append(value * (1.0 / total))
        tiles = (
            jnp.where(lanes < 96, outs[0], outs[1][:, :128]),
            jnp.where(lanes < 64, outs[1][:, 128:], outs[2][:, :128]),
            jnp.where(lanes < 32, outs[2][:, 128:], outs[3]),
        )
        for j, tile in enumerate(tiles):
            attended[:, pl.ds(pl.multiple_of(base + j * 128, 128), 128)] = tile.astype(BF)
        return carry

    lax.fori_loop(0, inner // (4 * HEAD), group, 0)
    for i in range(weight_ref.shape[1] // SPAN):
        there = slice(i * SPAN, (i + 1) * SPAN)
        update = gate_ref[:, there] * jnp.dot(
            attended[...], weight_ref[:, there], preferred_element_type=F32
        )
        done = 0
        for hidden_ref, out_ref in zip(hidden_refs, out_refs):
            count = hidden_ref.shape[0]
            part = update[done : done + count]
            out_ref[:, there] = (hidden_ref[:, there].astype(F32) + part).astype(BF)
            done += count


def attention(projected, text, bias, gate, weight, hidden, queries, after=()):
    hidden = [hidden[i] for i in queries]
    rows = sum(part.shape[0] for part in hidden)
    return pl.pallas_call(
        functools.partial(attention_kernel, queries=queries, blocks=len(projected)),
        in_specs=[whole()] * (len(projected) + 4 + len(hidden))
        + [pl.BlockSpec(memory_space=pl.ANY)] * len(after),
        cost_estimate=pl.CostEstimate(
            flops=4 * rows * weight.shape[0] * weight.shape[1],
            bytes_accessed=8 * 1024 * 1024,
            transcendentals=0,
        ),
        out_specs=[whole()] * len(hidden),
        out_shape=[jax.ShapeDtypeStruct(part.shape, BF) for part in hidden],
        scratch_shapes=[pltpu.VMEM((rows, weight.shape[0]), BF)],
        compiler_params=params(),
        name="attention",
    )(*projected, text, bias, gate, weight, *hidden, *after)


def on_device(
    latent_noise,
    text_rows,
    text_lengths,
    plan,
    context_weight,
    w_embed,
    w_attention,
    w_project,
    w_modulate,
    w_final,
):
    x, z, y, c = (lax.axis_index(name) for name in AXES)
    width = w_embed.shape[1]
    latent_width = latent_noise.shape[3]
    rows_here = latent_noise.shape[2]
    patches = rows_here * Z * Y
    text_total = text_rows.shape[2]
    core = jnp.reshape(c, (1,)).astype(jnp.int32)
    image = z // 2

    def across(value):
        return move(
            value, [((a, b, 0, 1 - b % C), (a, b, 0, b % C)) for a in range(X) for b in range(Z)]
        )

    def hop(value, source, target):
        return move(value, [((source, b, 0, d), (target, b, 0, d)) for _, b, d in homes()])

    levels = plan.astype(F32)
    mod_rows = w_modulate.shape[1]
    features = jnp.stack([time_features(levels[k], C * mod_rows) for k in range(STEPS)])
    features = lax.dynamic_slice_in_dim(features, c * mod_rows, mod_rows, 1)
    modulation = jnp.dot(features, w_modulate[0], preferred_element_type=F32)
    modulation = modulation + across(modulation)

    text = lax.dynamic_index_in_dim(text_rows[:, 0], x, 0, keepdims=False)
    partial = jnp.dot(text, context_weight, preferred_element_type=F32).astype(BF)
    attn_mine, proj_mine = w_attention[0], w_project[0]

    def beside(operand, piece):
        operand, piece = lax.optimization_barrier((operand, piece))
        return operand, across(piece)

    quarter = text_total // Y
    eighth = quarter // Z
    latent = latent_noise[0, 0].reshape(1, rows_here * latent_width)
    high = latent.astype(BF)
    low = (latent - high.astype(F32)).astype(BF)
    both = jnp.pad(jnp.concatenate([high, low], 0), ((0, 0), (0, width - latent.shape[1])))
    message = jnp.concatenate(
        [partial.reshape(Y, quarter, width), jnp.broadcast_to(both[None], (Y, 2, width))], 1
    )
    message, attn_piece = beside(message, attn_mine)
    parts = lax.all_to_all(message, "y", split_axis=0, concat_axis=0, tiled=True)
    summed = jnp.sum(parts[:, :quarter].astype(F32), axis=0).astype(BF)
    both = parts[:, quarter:].reshape(1, 2 * Y, width)
    message = jnp.concatenate(
        [summed.reshape(Z, eighth, width), jnp.broadcast_to(both, (Z, 2 * Y, width))], 1
    )
    parts = lax.all_to_all(message, "z", split_axis=0, concat_axis=0, tiled=True)
    both = parts[:, eighth:].reshape(patches // rows_here, 2, width)[:, :, : latent.shape[1]]
    both = jnp.transpose(both, (1, 0, 2)).reshape(2, patches * latent_width // 128, 128)

    def to_plane(value, plane):
        sent = move(value, [((m, b, 0, d), (plane, b, 0, d)) for m, b, d in homes() if m != plane])
        return jnp.where(image == plane, value, sent)

    first = to_plane(both[0], 0).reshape(patches, latent_width)
    latent = to_plane(both, BLOCKS - 1)
    latent = (latent[0].astype(F32) + latent[1].astype(F32)).reshape(patches, latent_width)
    length = jnp.sum(jnp.where(jnp.arange(X) == image, text_lengths[:, 0], 0))
    bias = jnp.where(jnp.arange(text_total) < length, 0.0, -1e30).astype(F32)[None, :]
    pace = (levels[1:] - levels[:-1]) / 1000.0
    shifts, scales, gates = (
        [modulation[k : k + 1, part * width : (part + 1) * width] for k in range(STEPS)]
        for part in range(3)
    )

    message = spread_over(parts, X, eighth)
    shared = lax.all_to_all(message, "x", split_axis=0, concat_axis=0, tiled=True)
    early = (first, latent, bias, w_final, w_embed, *shifts, *scales, *gates)
    message, piece = beside(twice(shared, Z, early), proj_mine)
    shared = lax.all_to_all(message, "z", split_axis=0, concat_axis=0, tiled=True)
    ready = (first, latent, bias, w_final, w_embed, *shifts, *scales, *gates)
    attn_weight = joined(core, attn_mine, [attn_piece], ready)
    hidden = embedded(first, w_embed)

    def products(hidden, step):
        done = []
        for part in hidden:
            done.append(
                product([part], attn_weight, 0, (shifts[step], scales[step]), tuple(done[-1:]))
            )
        return done

    projected = products(hidden, 0)
    pieces = [shared.reshape(quarter, width)]
    for k in range(1, Y):
        pieces.append(
            move(
                pieces[0],
                [((a, b, k, b % C), (a, b, 0, b % C)) for a in range(X) for b in range(Z)],
            )
        )
    proj_weight = joined(core, proj_mine, [piece], ready)
    keys = product(pieces, attn_weight, width)

    for turn in range(STEPS * BLOCKS):
        step, block = divmod(turn, BLOCKS)
        gate = gates[step]
        if turn > 0:
            projected = products(hidden, step)
        following = []
        for call in CALLS:
            queries = tuple(range(len(following), len(following) + len(call)))
            following = following + list(
                attention(
                    projected,
                    keys,
                    bias,
                    gate,
                    proj_weight,
                    hidden,
                    queries,
                    tuple(following[-1:]),
                )
            )
        hidden = following
        if block < BLOCKS - 1:
            hidden = [hop(part, block, block + 1) for part in hidden]
        else:
            latent, rounded = finished(pace, hidden, w_final, latent, step)
            if step < STEPS - 1:
                hidden = embedded(hop(rounded, block, 0), w_embed)

    last = BLOCKS - 1
    latent = latent.reshape(patches * latent_width // 128, 128)
    moved = move(latent, [((last, b, 0, d), (m, b, 0, d)) for m, b, d in homes() if m != last])
    latent = jnp.where(x == last, latent, moved)
    spread = lax.all_to_all(
        latent.reshape(Z * Y, rows_here * latent_width // 128, 128),
        ("z", "y"),
        split_axis=0,
        concat_axis=0,
        tiled=True,
    )
    mine = lax.dynamic_index_in_dim(spread, (2 * x + c) * Y, 0, keepdims=False)
    return mine.reshape(latent_noise.shape)


def solution(mesh):
    inner = Mesh(mesh.devices.reshape(X, Z, Y, C), AXES)
    seq = ("z", "y")
    placed = (
        P("x", "c", seq, None),
        P(None, "c", None, seq),
        P(None, "c"),
        P(),
        P(seq, None),
        P(),
        P("x", "c", None),
        P("x", "c", None),
        P("x", "c", None),
        P(),
    )
    return jax.shard_map(
        on_device,
        mesh=inner,
        in_specs=placed,
        out_specs=P("x", "c", seq, None),
        check_vma=False,
    )
```

```python
import functools
import math

import jax
import jax.numpy as jnp
from jax import lax
from jax.experimental import pallas as pl
from jax.experimental.pallas import tpu as pltpu
from jax.sharding import Mesh, PartitionSpec as P

HEADS = 16
HEAD = 96
STEPS = 2
BLOCKS = 4
X, Z, Y, C = 4, 8, 4, 2
AXES = ("x", "z", "y", "c")
BF = jnp.bfloat16
F32 = jnp.float32
VMEM = 20 * 1024 * 1024
SPAN = 768
CALLS = ((128, 128), (128, 128))
CHUNKS = sum(CALLS, ())

epsilon = 1e-06


def time_features(noise_level, feature_count):
    half_count = feature_count // 2
    wave_frequency = jnp.exp(
        -math.log(10000.0) * jnp.arange(half_count, dtype=F32) / half_count
    )
    angles = noise_level * wave_frequency
    return jnp.concatenate([jnp.cos(angles), jnp.sin(angles)]).astype(BF)


def flat(x, z, y, c):
    return ((x * Z + z) * Y + y) * C + c


def move(value, pairs):
    return lax.ppermute(value, AXES, [(flat(*a), flat(*b)) for a, b in pairs])


def homes():
    return [(z // 2, z, z % 2) for z in range(Z)]


def whole():
    return pl.BlockSpec(memory_space=pltpu.VMEM)


def scalar():
    return pl.BlockSpec(memory_space=pltpu.SMEM)


def params():
    return pltpu.CompilerParams(vmem_limit_bytes=VMEM)


def joined_kernel(core_ref, own_ref, *refs, pieces):
    piece_refs, (out_ref, sems) = refs[:pieces], refs[-2:]
    half = own_ref.shape[0]
    core = core_ref[0]

    def target(start, count):
        return out_ref.at[pl.ds(pl.multiple_of(start, 16), count), :]

    copies = [pltpu.make_async_copy(own_ref, target(core * half, half), sems.at[0])]
    done = 0
    for k, ref in enumerate(piece_refs):
        count = ref.shape[0]
        copies.append(
            pltpu.make_async_copy(ref, target((1 - core) * half + done, count), sems.at[k + 1])
        )
        done += count
    for copy in copies:
        copy.start()
    for copy in copies:
        copy.wait()


def joined(core, own, pieces, after):
    half, columns = own.shape
    return pl.pallas_call(
        functools.partial(joined_kernel, pieces=len(pieces)),
        in_specs=[scalar()]
        + [pl.BlockSpec(memory_space=pltpu.HBM)] * (1 + len(pieces))
        + [pl.BlockSpec(memory_space=pl.ANY)] * len(after),
        out_specs=whole(),
        out_shape=jax.ShapeDtypeStruct((2 * half, columns), BF),
        scratch_shapes=[pltpu.SemaphoreType.DMA((1 + len(pieces),))],
        compiler_params=params(),
        cost_estimate=pl.CostEstimate(flops=0, bytes_accessed=1024, transcendentals=0),
        name="joined",
    )(core, own, *pieces, *after)


def normal(values):
    center = values - jnp.mean(values, axis=-1, keepdims=True)
    spread = jnp.mean(center * center, axis=-1, keepdims=True)
    return center * lax.rsqrt(spread + epsilon)


def product_kernel(*refs, pieces, column):
    row_refs, refs = refs[:pieces], refs[pieces:]
    weight_ref, refs = refs[0], refs[1:]
    out_ref, source = refs[-2:]
    done = 0
    for ref in row_refs:
        count = ref.shape[0]
        for i in range(0, count, 64):
            values = ref[i : i + 64, :]
            if column == 0:
                shift_ref, scale_ref = refs[:2]
                values = normal(values.astype(F32))
                values = (values * (1.0 + scale_ref[...]) + shift_ref[...]).astype(BF)
            source[done + i : done + i + 64, :] = values
        done += count
    for i in range(out_ref.shape[1] // SPAN):
        there = slice(i * SPAN, (i + 1) * SPAN)
        here = slice(column + i * SPAN, column + (i + 1) * SPAN)
        out_ref[:, there] = jnp.dot(
            source[...], weight_ref[:, here], preferred_element_type=F32
        ).astype(BF)


def product(rows, weight, column, modulate=(), after=()):
    count = sum(part.shape[0] for part in rows)
    width = weight.shape[0]
    columns = weight.shape[1] - column
    return pl.pallas_call(
        functools.partial(product_kernel, pieces=len(rows), column=column),
        in_specs=[whole()] * (len(rows) + 1 + len(modulate))
        + [pl.BlockSpec(memory_space=pl.ANY)] * len(after),
        out_specs=whole(),
        out_shape=jax.ShapeDtypeStruct((count, columns), BF),
        cost_estimate=pl.CostEstimate(
            flops=2 * count * width * columns,
            bytes_accessed=2 * 1024 * 1024,
            transcendentals=0,
        ),
        scratch_shapes=[pltpu.VMEM((count, width), BF)],
        compiler_params=params(),
        name="product",
    )(*rows, weight, *modulate, *after)


def embed_kernel(latent_ref, weight_ref, *out_refs):
    done = 0
    for ref in out_refs:
        count = ref.shape[0]
        ref[...] = jnp.dot(
            latent_ref[done : done + count, :], weight_ref[...], preferred_element_type=F32
        ).astype(BF)
        done += count


def embedded(latent, weight):
    return pl.pallas_call(
        embed_kernel,
        in_specs=[whole()] * 2,
        out_specs=[whole()] * len(CHUNKS),
        out_shape=[jax.ShapeDtypeStruct((rows, weight.shape[1]), BF) for rows in CHUNKS],
        compiler_params=params(),
        name="embed",
    )(latent, weight)


def finish_kernel(pace_ref, *refs, step):
    *row_refs, weight_ref, latent_ref, out_ref, rounded_ref = refs
    pace = pace_ref[step]
    done = 0
    for ref in row_refs:
        count = ref.shape[0]
        there = slice(done, done + count)
        velocity = jnp.dot(
            normal(ref[...].astype(F32)).astype(BF),
            weight_ref[...],
            preferred_element_type=F32,
        )
        latent = latent_ref[there, :] + pace * velocity
        out_ref[there, :] = latent
        rounded_ref[there, :] = latent.astype(BF)
        done += count


def finished(pace, hidden, weight, latent, step):
    return pl.pallas_call(
        functools.partial(finish_kernel, step=step),
        in_specs=[scalar()] + [whole()] * (len(hidden) + 2),
        out_specs=[whole()] * 2,
        out_shape=[
            jax.ShapeDtypeStruct(latent.shape, F32),
            jax.ShapeDtypeStruct(latent.shape, BF),
        ],
        compiler_params=params(),
        name="finish",
    )(pace, *hidden, weight, latent)


def spread_kernel(parts_ref, out_ref):
    count = out_ref.shape[1]
    total = parts_ref[0, :count].astype(F32)
    for k in range(1, parts_ref.shape[0]):
        total = total + parts_ref[k, :count].astype(F32)
    for k in range(out_ref.shape[0]):
        out_ref[k] = total.astype(BF)


def spread_over(parts, copies, count):
    return pl.pallas_call(
        spread_kernel,
        in_specs=[whole()],
        out_specs=whole(),
        out_shape=jax.ShapeDtypeStruct((copies, count, parts.shape[2]), BF),
        compiler_params=params(),
        name="spread",
    )(parts)


def twice_kernel(rows_ref, *refs):
    out_ref = refs[-1]
    for k in range(out_ref.shape[0]):
        out_ref[k] = rows_ref[k * rows_ref.shape[0] // out_ref.shape[0]]


def twice(rows, copies, after):
    return pl.pallas_call(
        twice_kernel,
        in_specs=[whole()] + [pl.BlockSpec(memory_space=pl.ANY)] * len(after),
        out_specs=whole(),
        out_shape=jax.ShapeDtypeStruct((copies,) + rows.shape[1:], BF),
        compiler_params=params(),
        name="twice",
    )(rows, *after)


def attention_kernel(*refs, queries, blocks):
    projected, refs = refs[:blocks], refs[blocks:]
    text_ref, bias_ref, gate_ref, weight_ref, *refs = refs
    count = len(queries)
    hidden_refs, out_refs, attended = refs[:count], refs[-count - 1 : -1], refs[-1]
    inner = weight_ref.shape[0]
    factor = math.log2(math.e) / math.sqrt(HEAD)
    lanes = lax.broadcasted_iota(jnp.int32, (1, 128), 1)
    wide = lax.broadcasted_iota(jnp.int32, (1, 256), 1)
    bias = bias_ref[...]
    contract = (((1,), (1,)), ((), ()))

    def group(g, carry):
        base = pl.multiple_of(g * 4 * HEAD, 128)
        outs = []
        for h in range(4):
            low, high = h * HEAD, (h + 1) * HEAD
            start, stop = low // 128 * 128, -(-high // 128) * 128
            width = stop - start

            def window(refs, offset):
                there = pl.ds(pl.multiple_of(base + start + offset, 128), width)
                return jnp.concatenate([ref[:, there] for ref in refs], 0)

            index = lanes if width == 128 else wide
            mask = ((index >= low - start) & (index < high - start)).astype(F32).astype(BF)
            q = window([projected[i] for i in queries], 0) * mask
            image = lax.dot_general(
                q, window(projected, inner), contract, preferred_element_type=F32
            )
            text = lax.dot_general(
                q, window([text_ref], 0), contract, preferred_element_type=F32
            )
            text = text + bias
            top = jnp.maximum(
                jnp.max(image, axis=-1, keepdims=True), jnp.max(text, axis=-1, keepdims=True)
            )
            image = jnp.exp2((image - top) * factor)
            text = jnp.exp2((text - top) * factor)
            total = jnp.sum(image, axis=-1, keepdims=True) + jnp.sum(text, axis=-1, keepdims=True)
            value = jnp.dot(
                image.astype(BF), window(projected, 2 * inner), preferred_element_type=F32
            ) + jnp.dot(
                text.astype(BF), window([text_ref], inner), preferred_element_type=F32
            )
            outs.append(value * (1.0 / total))
        tiles = (
            jnp.where(lanes < 96, outs[0], outs[1][:, :128]),
            jnp.where(lanes < 64, outs[1][:, 128:], outs[2][:, :128]),
            jnp.where(lanes < 32, outs[2][:, 128:], outs[3]),
        )
        for j, tile in enumerate(tiles):
            attended[:, pl.ds(pl.multiple_of(base + j * 128, 128), 128)] = tile.astype(BF)
        return carry

    lax.fori_loop(0, inner // (4 * HEAD), group, 0)
    for i in range(weight_ref.shape[1] // SPAN):
        there = slice(i * SPAN, (i + 1) * SPAN)
        update = gate_ref[:, there] * jnp.dot(
            attended[...], weight_ref[:, there], preferred_element_type=F32
        )
        done = 0
        for hidden_ref, out_ref in zip(hidden_refs, out_refs):
            count = hidden_ref.shape[0]
            part = update[done : done + count]
            out_ref[:, there] = (hidden_ref[:, there].astype(F32) + part).astype(BF)
            done += count


def attention(projected, text, bias, gate, weight, hidden, queries, after=()):
    hidden = [hidden[i] for i in queries]
    rows = sum(part.shape[0] for part in hidden)
    return pl.pallas_call(
        functools.partial(attention_kernel, queries=queries, blocks=len(projected)),
        in_specs=[whole()] * (len(projected) + 4 + len(hidden))
        + [pl.BlockSpec(memory_space=pl.ANY)] * len(after),
        cost_estimate=pl.CostEstimate(
            flops=4 * rows * weight.shape[0] * weight.shape[1],
            bytes_accessed=8 * 1024 * 1024,
            transcendentals=0,
        ),
        out_specs=[whole()] * len(hidden),
        out_shape=[jax.ShapeDtypeStruct(part.shape, BF) for part in hidden],
        scratch_shapes=[pltpu.VMEM((rows, weight.shape[0]), BF)],
        compiler_params=params(),
        name="attention",
    )(*projected, text, bias, gate, weight, *hidden, *after)


def on_device(
    latent_noise,
    text_rows,
    text_lengths,
    plan,
    context_weight,
    w_embed,
    w_attention,
    w_project,
    w_modulate,
    w_final,
):
    x, z, y, c = (lax.axis_index(name) for name in AXES)
    width = w_embed.shape[1]
    latent_width = latent_noise.shape[3]
    rows_here = latent_noise.shape[2]
    patches = rows_here * Z * Y
    text_total = text_rows.shape[2]
    core = jnp.reshape(c, (1,)).astype(jnp.int32)
    image = z // 2

    def across(value):
        return move(
            value, [((a, b, 0, 1 - b % C), (a, b, 0, b % C)) for a in range(X) for b in range(Z)]
        )

    def hop(value, source, target):
        return move(value, [((source, b, 0, d), (target, b, 0, d)) for _, b, d in homes()])

    levels = plan.astype(F32)
    mod_rows = w_modulate.shape[1]
    features = jnp.stack([time_features(levels[k], C * mod_rows) for k in range(STEPS)])
    features = lax.dynamic_slice_in_dim(features, c * mod_rows, mod_rows, 1)
    modulation = jnp.dot(features, w_modulate[0], preferred_element_type=F32)
    modulation = modulation + across(modulation)

    text = lax.dynamic_index_in_dim(text_rows[:, 0], x, 0, keepdims=False)
    partial = jnp.dot(text, context_weight, preferred_element_type=F32).astype(BF)
    attn_mine, proj_mine = w_attention[0], w_project[0]

    def beside(operand, piece):
        operand, piece = lax.optimization_barrier((operand, piece))
        return operand, across(piece)

    quarter = text_total // Y
    eighth = quarter // Z
    latent = latent_noise[0, 0].reshape(1, rows_here * latent_width)
    high = latent.astype(BF)
    low = (latent - high.astype(F32)).astype(BF)
    both = jnp.pad(jnp.concatenate([high, low], 0), ((0, 0), (0, width - latent.shape[1])))
    message = jnp.concatenate(
        [partial.reshape(Y, quarter, width), jnp.broadcast_to(both[None], (Y, 2, width))], 1
    )
    parts = lax.all_to_all(message, "y", split_axis=0, concat_axis=0, tiled=True)
    summed = jnp.sum(parts[:, :quarter].astype(F32), axis=0).astype(BF)
    both = parts[:, quarter:].reshape(1, 2 * Y, width)
    message = jnp.concatenate(
        [summed.reshape(Z, eighth, width), jnp.broadcast_to(both, (Z, 2 * Y, width))], 1
    )
    message, attn_piece = beside(message, attn_mine)
    parts = lax.all_to_all(message, "z", split_axis=0, concat_axis=0, tiled=True)
    both = parts[:, eighth:].reshape(patches // rows_here, 2, width)[:, :, : latent.shape[1]]
    both = jnp.transpose(both, (1, 0, 2)).reshape(2, patches * latent_width // 128, 128)

    def to_plane(value, plane):
        sent = move(value, [((m, b, 0, d), (plane, b, 0, d)) for m, b, d in homes() if m != plane])
        return jnp.where(image == plane, value, sent)

    first = to_plane(both[0], 0).reshape(patches, latent_width)
    latent = to_plane(both, BLOCKS - 1)
    latent = (latent[0].astype(F32) + latent[1].astype(F32)).reshape(patches, latent_width)
    length = jnp.sum(jnp.where(jnp.arange(X) == image, text_lengths[:, 0], 0))
    bias = jnp.where(jnp.arange(text_total) < length, 0.0, -1e30).astype(F32)[None, :]
    pace = (levels[1:] - levels[:-1]) / 1000.0
    shifts, scales, gates = (
        [modulation[k : k + 1, part * width : (part + 1) * width] for k in range(STEPS)]
        for part in range(3)
    )

    message = spread_over(parts, X, eighth)
    shared = lax.all_to_all(message, "x", split_axis=0, concat_axis=0, tiled=True)
    early = (first, latent, bias, w_final, w_embed, *shifts, *scales, *gates)
    message, piece = beside(twice(shared, Z, early), proj_mine)
    shared = lax.all_to_all(message, "z", split_axis=0, concat_axis=0, tiled=True)
    ready = (first, latent, bias, w_final, w_embed, *shifts, *scales, *gates)
    attn_weight = joined(core, attn_mine, [attn_piece], ready)
    hidden = embedded(first, w_embed)

    def products(hidden, step):
        done = []
        for part in hidden:
            done.append(
                product([part], attn_weight, 0, (shifts[step], scales[step]), tuple(done[-1:]))
            )
        return done

    projected = products(hidden, 0)
    pieces = [shared.reshape(quarter, width)]
    for k in range(1, Y):
        pieces.append(
            move(
                pieces[0],
                [((a, b, k, b % C), (a, b, 0, b % C)) for a in range(X) for b in range(Z)],
            )
        )
    proj_weight = joined(core, proj_mine, [piece], ready)
    keys = product(pieces, attn_weight, width)

    for turn in range(STEPS * BLOCKS):
        step, block = divmod(turn, BLOCKS)
        gate = gates[step]
        if turn > 0:
            projected = products(hidden, step)
        following = []
        for call in CALLS:
            queries = tuple(range(len(following), len(following) + len(call)))
            following = following + list(
                attention(
                    projected,
                    keys,
                    bias,
                    gate,
                    proj_weight,
                    hidden,
                    queries,
                    tuple(following[-1:]),
                )
            )
        hidden = following
        if block < BLOCKS - 1:
            hidden = [hop(part, block, block + 1) for part in hidden]
        else:
            latent, rounded = finished(pace, hidden, w_final, latent, step)
            if step < STEPS - 1:
                hidden = embedded(hop(rounded, block, 0), w_embed)

    last = BLOCKS - 1
    latent = latent.reshape(patches * latent_width // 128, 128)
    moved = move(latent, [((last, b, 0, d), (m, b, 0, d)) for m, b, d in homes() if m != last])
    latent = jnp.where(x == last, latent, moved)
    spread = lax.all_to_all(
        latent.reshape(Z * Y, rows_here * latent_width // 128, 128),
        ("z", "y"),
        split_axis=0,
        concat_axis=0,
        tiled=True,
    )
    mine = lax.dynamic_index_in_dim(spread, (2 * x + c) * Y, 0, keepdims=False)
    return mine.reshape(latent_noise.shape)


def solution(mesh):
    inner = Mesh(mesh.devices.reshape(X, Z, Y, C), AXES)
    seq = ("z", "y")
    placed = (
        P("x", "c", seq, None),
        P(None, "c", None, seq),
        P(None, "c"),
        P(),
        P(seq, None),
        P(),
        P("x", "c", None),
        P("x", "c", None),
        P("x", "c", None),
        P(),
    )
    return jax.shard_map(
        on_device,
        mesh=inner,
        in_specs=placed,
        out_specs=P("x", "c", seq, None),
        check_vma=False,
    )
```

```python
import functools
import math

import jax
import jax.numpy as jnp
from jax import lax
from jax.experimental import pallas as pl
from jax.experimental.pallas import tpu as pltpu
from jax.sharding import Mesh, PartitionSpec as P

HEADS = 16
HEAD = 96
STEPS = 2
BLOCKS = 4
X, Z, Y, C = 4, 8, 4, 2
AXES = ("x", "z", "y", "c")
BF = jnp.bfloat16
F32 = jnp.float32
VMEM = 20 * 1024 * 1024
SPAN = 768
CALLS = ((256,), (128, 128))
CHUNKS = sum(CALLS, ())

epsilon = 1e-06


def time_features(noise_level, feature_count):
    half_count = feature_count // 2
    wave_frequency = jnp.exp(
        -math.log(10000.0) * jnp.arange(half_count, dtype=F32) / half_count
    )
    angles = noise_level * wave_frequency
    return jnp.concatenate([jnp.cos(angles), jnp.sin(angles)]).astype(BF)


def flat(x, z, y, c):
    return ((x * Z + z) * Y + y) * C + c


def move(value, pairs):
    return lax.ppermute(value, AXES, [(flat(*a), flat(*b)) for a, b in pairs])


def homes():
    return [(z // 2, z, z % 2) for z in range(Z)]


def whole():
    return pl.BlockSpec(memory_space=pltpu.VMEM)


def scalar():
    return pl.BlockSpec(memory_space=pltpu.SMEM)


def params():
    return pltpu.CompilerParams(vmem_limit_bytes=VMEM)


def joined_kernel(core_ref, own_ref, *refs, pieces):
    piece_refs, (out_ref, sems) = refs[:pieces], refs[-2:]
    half = own_ref.shape[0]
    core = core_ref[0]

    def target(start, count):
        return out_ref.at[pl.ds(pl.multiple_of(start, 16), count), :]

    copies = [pltpu.make_async_copy(own_ref, target(core * half, half), sems.at[0])]
    done = 0
    for k, ref in enumerate(piece_refs):
        count = ref.shape[0]
        copies.append(
            pltpu.make_async_copy(ref, target((1 - core) * half + done, count), sems.at[k + 1])
        )
        done += count
    for copy in copies:
        copy.start()
    for copy in copies:
        copy.wait()


def joined(core, own, pieces, after):
    half, columns = own.shape
    return pl.pallas_call(
        functools.partial(joined_kernel, pieces=len(pieces)),
        in_specs=[scalar()]
        + [pl.BlockSpec(memory_space=pltpu.HBM)] * (1 + len(pieces))
        + [pl.BlockSpec(memory_space=pl.ANY)] * len(after),
        out_specs=whole(),
        out_shape=jax.ShapeDtypeStruct((2 * half, columns), BF),
        scratch_shapes=[pltpu.SemaphoreType.DMA((1 + len(pieces),))],
        compiler_params=params(),
        cost_estimate=pl.CostEstimate(flops=0, bytes_accessed=1024, transcendentals=0),
        name="joined",
    )(core, own, *pieces, *after)


def normal(values):
    center = values - jnp.mean(values, axis=-1, keepdims=True)
    spread = jnp.mean(center * center, axis=-1, keepdims=True)
    return center * lax.rsqrt(spread + epsilon)


def product_kernel(*refs, pieces, column):
    row_refs, refs = refs[:pieces], refs[pieces:]
    weight_ref, refs = refs[0], refs[1:]
    out_ref, source = refs[-2:]
    done = 0
    for ref in row_refs:
        count = ref.shape[0]
        for i in range(0, count, 64):
            values = ref[i : i + 64, :]
            if column == 0:
                shift_ref, scale_ref = refs[:2]
                values = normal(values.astype(F32))
                values = (values * (1.0 + scale_ref[...]) + shift_ref[...]).astype(BF)
            source[done + i : done + i + 64, :] = values
        done += count
    for i in range(out_ref.shape[1] // SPAN):
        there = slice(i * SPAN, (i + 1) * SPAN)
        here = slice(column + i * SPAN, column + (i + 1) * SPAN)
        out_ref[:, there] = jnp.dot(
            source[...], weight_ref[:, here], preferred_element_type=F32
        ).astype(BF)


def product(rows, weight, column, modulate=(), after=()):
    count = sum(part.shape[0] for part in rows)
    width = weight.shape[0]
    columns = weight.shape[1] - column
    return pl.pallas_call(
        functools.partial(product_kernel, pieces=len(rows), column=column),
        in_specs=[whole()] * (len(rows) + 1 + len(modulate))
        + [pl.BlockSpec(memory_space=pl.ANY)] * len(after),
        out_specs=whole(),
        out_shape=jax.ShapeDtypeStruct((count, columns), BF),
        cost_estimate=pl.CostEstimate(
            flops=2 * count * width * columns,
            bytes_accessed=2 * 1024 * 1024,
            transcendentals=0,
        ),
        scratch_shapes=[pltpu.VMEM((count, width), BF)],
        compiler_params=params(),
        name="product",
    )(*rows, weight, *modulate, *after)


def embed_kernel(latent_ref, weight_ref, *out_refs):
    done = 0
    for ref in out_refs:
        count = ref.shape[0]
        ref[...] = jnp.dot(
            latent_ref[done : done + count, :], weight_ref[...], preferred_element_type=F32
        ).astype(BF)
        done += count


def embedded(latent, weight):
    return pl.pallas_call(
        embed_kernel,
        in_specs=[whole()] * 2,
        out_specs=[whole()] * len(CHUNKS),
        out_shape=[jax.ShapeDtypeStruct((rows, weight.shape[1]), BF) for rows in CHUNKS],
        compiler_params=params(),
        name="embed",
    )(latent, weight)


def finish_kernel(pace_ref, *refs, step):
    *row_refs, weight_ref, latent_ref, out_ref, rounded_ref = refs
    pace = pace_ref[step]
    done = 0
    for ref in row_refs:
        count = ref.shape[0]
        there = slice(done, done + count)
        velocity = jnp.dot(
            normal(ref[...].astype(F32)).astype(BF),
            weight_ref[...],
            preferred_element_type=F32,
        )
        latent = latent_ref[there, :] + pace * velocity
        out_ref[there, :] = latent
        rounded_ref[there, :] = latent.astype(BF)
        done += count


def finished(pace, hidden, weight, latent, step):
    return pl.pallas_call(
        functools.partial(finish_kernel, step=step),
        in_specs=[scalar()] + [whole()] * (len(hidden) + 2),
        out_specs=[whole()] * 2,
        out_shape=[
            jax.ShapeDtypeStruct(latent.shape, F32),
            jax.ShapeDtypeStruct(latent.shape, BF),
        ],
        compiler_params=params(),
        name="finish",
    )(pace, *hidden, weight, latent)


def spread_kernel(parts_ref, out_ref):
    count = out_ref.shape[1]
    total = parts_ref[0, :count].astype(F32)
    for k in range(1, parts_ref.shape[0]):
        total = total + parts_ref[k, :count].astype(F32)
    for k in range(out_ref.shape[0]):
        out_ref[k] = total.astype(BF)


def spread_over(parts, copies, count):
    return pl.pallas_call(
        spread_kernel,
        in_specs=[whole()],
        out_specs=whole(),
        out_shape=jax.ShapeDtypeStruct((copies, count, parts.shape[2]), BF),
        compiler_params=params(),
        name="spread",
    )(parts)


def twice_kernel(rows_ref, *refs):
    out_ref = refs[-1]
    for k in range(out_ref.shape[0]):
        out_ref[k] = rows_ref[k * rows_ref.shape[0] // out_ref.shape[0]]


def twice(rows, copies, after):
    return pl.pallas_call(
        twice_kernel,
        in_specs=[whole()] + [pl.BlockSpec(memory_space=pl.ANY)] * len(after),
        out_specs=whole(),
        out_shape=jax.ShapeDtypeStruct((copies,) + rows.shape[1:], BF),
        compiler_params=params(),
        name="twice",
    )(rows, *after)


def attention_kernel(*refs, queries, blocks):
    projected, refs = refs[:blocks], refs[blocks:]
    text_ref, bias_ref, gate_ref, weight_ref, *refs = refs
    count = len(queries)
    hidden_refs, out_refs, attended = refs[:count], refs[-count - 1 : -1], refs[-1]
    inner = weight_ref.shape[0]
    factor = math.log2(math.e) / math.sqrt(HEAD)
    lanes = lax.broadcasted_iota(jnp.int32, (1, 128), 1)
    wide = lax.broadcasted_iota(jnp.int32, (1, 256), 1)
    bias = bias_ref[...]
    contract = (((1,), (1,)), ((), ()))

    def group(g, carry):
        base = pl.multiple_of(g * 4 * HEAD, 128)
        outs = []
        for h in range(4):
            low, high = h * HEAD, (h + 1) * HEAD
            start, stop = low // 128 * 128, -(-high // 128) * 128
            width = stop - start

            def window(refs, offset):
                there = pl.ds(pl.multiple_of(base + start + offset, 128), width)
                return jnp.concatenate([ref[:, there] for ref in refs], 0)

            index = lanes if width == 128 else wide
            mask = ((index >= low - start) & (index < high - start)).astype(F32).astype(BF)
            q = window([projected[i] for i in queries], 0) * mask
            image = lax.dot_general(
                q, window(projected, inner), contract, preferred_element_type=F32
            )
            text = lax.dot_general(
                q, window([text_ref], 0), contract, preferred_element_type=F32
            )
            text = text + bias
            top = jnp.maximum(
                jnp.max(image, axis=-1, keepdims=True), jnp.max(text, axis=-1, keepdims=True)
            )
            image = jnp.exp2((image - top) * factor)
            text = jnp.exp2((text - top) * factor)
            total = jnp.sum(image, axis=-1, keepdims=True) + jnp.sum(text, axis=-1, keepdims=True)
            value = jnp.dot(
                image.astype(BF), window(projected, 2 * inner), preferred_element_type=F32
            ) + jnp.dot(
                text.astype(BF), window([text_ref], inner), preferred_element_type=F32
            )
            outs.append(value * (1.0 / total))
        tiles = (
            jnp.where(lanes < 96, outs[0], outs[1][:, :128]),
            jnp.where(lanes < 64, outs[1][:, 128:], outs[2][:, :128]),
            jnp.where(lanes < 32, outs[2][:, 128:], outs[3]),
        )
        for j, tile in enumerate(tiles):
            attended[:, pl.ds(pl.multiple_of(base + j * 128, 128), 128)] = tile.astype(BF)
        return carry

    lax.fori_loop(0, inner // (4 * HEAD), group, 0)
    for i in range(weight_ref.shape[1] // SPAN):
        there = slice(i * SPAN, (i + 1) * SPAN)
        update = gate_ref[:, there] * jnp.dot(
            attended[...], weight_ref[:, there], preferred_element_type=F32
        )
        done = 0
        for hidden_ref, out_ref in zip(hidden_refs, out_refs):
            count = hidden_ref.shape[0]
            part = update[done : done + count]
            out_ref[:, there] = (hidden_ref[:, there].astype(F32) + part).astype(BF)
            done += count


def attention(projected, text, bias, gate, weight, hidden, queries, after=()):
    hidden = [hidden[i] for i in queries]
    rows = sum(part.shape[0] for part in hidden)
    return pl.pallas_call(
        functools.partial(attention_kernel, queries=queries, blocks=len(projected)),
        in_specs=[whole()] * (len(projected) + 4 + len(hidden))
        + [pl.BlockSpec(memory_space=pl.ANY)] * len(after),
        cost_estimate=pl.CostEstimate(
            flops=4 * rows * weight.shape[0] * weight.shape[1],
            bytes_accessed=8 * 1024 * 1024,
            transcendentals=0,
        ),
        out_specs=[whole()] * len(hidden),
        out_shape=[jax.ShapeDtypeStruct(part.shape, BF) for part in hidden],
        scratch_shapes=[pltpu.VMEM((rows, weight.shape[0]), BF)],
        compiler_params=params(),
        name="attention",
    )(*projected, text, bias, gate, weight, *hidden, *after)


def on_device(
    latent_noise,
    text_rows,
    text_lengths,
    plan,
    context_weight,
    w_embed,
    w_attention,
    w_project,
    w_modulate,
    w_final,
):
    x, z, y, c = (lax.axis_index(name) for name in AXES)
    width = w_embed.shape[1]
    latent_width = latent_noise.shape[3]
    rows_here = latent_noise.shape[2]
    patches = rows_here * Z * Y
    text_total = text_rows.shape[2]
    core = jnp.reshape(c, (1,)).astype(jnp.int32)
    image = z // 2

    def across(value):
        return move(
            value, [((a, b, 0, 1 - b % C), (a, b, 0, b % C)) for a in range(X) for b in range(Z)]
        )

    def hop(value, source, target):
        return move(value, [((source, b, 0, d), (target, b, 0, d)) for _, b, d in homes()])

    levels = plan.astype(F32)
    mod_rows = w_modulate.shape[1]
    features = jnp.stack([time_features(levels[k], C * mod_rows) for k in range(STEPS)])
    features = lax.dynamic_slice_in_dim(features, c * mod_rows, mod_rows, 1)
    modulation = jnp.dot(features, w_modulate[0], preferred_element_type=F32)
    modulation = modulation + across(modulation)

    text = lax.dynamic_index_in_dim(text_rows[:, 0], x, 0, keepdims=False)
    partial = jnp.dot(text, context_weight, preferred_element_type=F32).astype(BF)
    attn_mine, proj_mine = w_attention[0], w_project[0]

    def beside(operand, piece):
        operand, piece = lax.optimization_barrier((operand, piece))
        return operand, across(piece)

    quarter = text_total // Y
    eighth = quarter // Z
    latent = latent_noise[0, 0].reshape(1, rows_here * latent_width)
    high = latent.astype(BF)
    low = (latent - high.astype(F32)).astype(BF)
    both = jnp.pad(jnp.concatenate([high, low], 0), ((0, 0), (0, width - latent.shape[1])))
    message = jnp.concatenate(
        [partial.reshape(Y, quarter, width), jnp.broadcast_to(both[None], (Y, 2, width))], 1
    )
    parts = lax.all_to_all(message, "y", split_axis=0, concat_axis=0, tiled=True)
    summed = jnp.sum(parts[:, :quarter].astype(F32), axis=0).astype(BF)
    both = parts[:, quarter:].reshape(1, 2 * Y, width)
    message = jnp.concatenate(
        [summed.reshape(Z, eighth, width), jnp.broadcast_to(both, (Z, 2 * Y, width))], 1
    )
    message, attn_piece = beside(message, attn_mine)
    parts = lax.all_to_all(message, "z", split_axis=0, concat_axis=0, tiled=True)
    both = parts[:, eighth:].reshape(patches // rows_here, 2, width)[:, :, : latent.shape[1]]
    both = jnp.transpose(both, (1, 0, 2)).reshape(2, patches * latent_width // 128, 128)

    def to_plane(value, plane):
        sent = move(value, [((m, b, 0, d), (plane, b, 0, d)) for m, b, d in homes() if m != plane])
        return jnp.where(image == plane, value, sent)

    first = to_plane(both[0], 0).reshape(patches, latent_width)
    latent = to_plane(both, BLOCKS - 1)
    latent = (latent[0].astype(F32) + latent[1].astype(F32)).reshape(patches, latent_width)
    length = jnp.sum(jnp.where(jnp.arange(X) == image, text_lengths[:, 0], 0))
    bias = jnp.where(jnp.arange(text_total) < length, 0.0, -1e30).astype(F32)[None, :]
    pace = (levels[1:] - levels[:-1]) / 1000.0
    shifts, scales, gates = (
        [modulation[k : k + 1, part * width : (part + 1) * width] for k in range(STEPS)]
        for part in range(3)
    )

    message = spread_over(parts, X, eighth)
    shared = lax.all_to_all(message, "x", split_axis=0, concat_axis=0, tiled=True)
    early = (first, latent, bias, w_final, w_embed, *shifts, *scales, *gates)
    message, piece = beside(twice(shared, Z, early), proj_mine)
    shared = lax.all_to_all(message, "z", split_axis=0, concat_axis=0, tiled=True)
    ready = (first, latent, bias, w_final, w_embed, *shifts, *scales, *gates)
    attn_weight = joined(core, attn_mine, [attn_piece], ready)
    hidden = embedded(first, w_embed)

    def products(hidden, step):
        done = []
        for part in hidden:
            done.append(
                product([part], attn_weight, 0, (shifts[step], scales[step]), tuple(done[-1:]))
            )
        return done

    projected = products(hidden, 0)
    pieces = [shared.reshape(quarter, width)]
    for k in range(1, Y):
        pieces.append(
            move(
                pieces[0],
                [((a, b, k, b % C), (a, b, 0, b % C)) for a in range(X) for b in range(Z)],
            )
        )
    proj_weight = joined(core, proj_mine, [piece], ready)
    keys = product(pieces, attn_weight, width)

    for turn in range(STEPS * BLOCKS):
        step, block = divmod(turn, BLOCKS)
        gate = gates[step]
        if turn > 0:
            projected = products(hidden, step)
        following = []
        for call in CALLS:
            queries = tuple(range(len(following), len(following) + len(call)))
            following = following + list(
                attention(
                    projected,
                    keys,
                    bias,
                    gate,
                    proj_weight,
                    hidden,
                    queries,
                    tuple(following[-1:]),
                )
            )
        hidden = following
        if block < BLOCKS - 1:
            hidden = [hop(part, block, block + 1) for part in hidden]
        else:
            latent, rounded = finished(pace, hidden, w_final, latent, step)
            if step < STEPS - 1:
                hidden = embedded(hop(rounded, block, 0), w_embed)

    last = BLOCKS - 1
    latent = latent.reshape(patches * latent_width // 128, 128)
    moved = move(latent, [((last, b, 0, d), (m, b, 0, d)) for m, b, d in homes() if m != last])
    latent = jnp.where(x == last, latent, moved)
    spread = lax.all_to_all(
        latent.reshape(Z * Y, rows_here * latent_width // 128, 128),
        ("z", "y"),
        split_axis=0,
        concat_axis=0,
        tiled=True,
    )
    mine = lax.dynamic_index_in_dim(spread, (2 * x + c) * Y, 0, keepdims=False)
    return mine.reshape(latent_noise.shape)


def solution(mesh):
    inner = Mesh(mesh.devices.reshape(X, Z, Y, C), AXES)
    seq = ("z", "y")
    placed = (
        P("x", "c", seq, None),
        P(None, "c", None, seq),
        P(None, "c"),
        P(),
        P(seq, None),
        P(),
        P("x", "c", None),
        P("x", "c", None),
        P("x", "c", None),
        P(),
    )
    return jax.shard_map(
        on_device,
        mesh=inner,
        in_specs=placed,
        out_specs=P("x", "c", seq, None),
        check_vma=False,
    )
```
